256 devices in a mesh: src: 16 (over x, y_lo, core), rcv: 16 (over z, y_hi).
Axes of the slice: x: 4, y: 4 (y_hi: 2, y_lo: 2; y = y_hi * 2 + y_lo), z: 8, core: 2. Of those that a mesh axis runs over, the one named last changes fastest.
Arguments:
- records: float32 [2048, 20480], P(('rcv', 'src')), may hold values from -500 to 500
- starts: int32 [2], replicated, may hold values from 0 to 10180, as said below
- block_mask: int32 [16, 16, 16], P('rcv', None, 'src'), may hold values from 0 to 1, as said below
Outputs:
- stacked: bfloat16 [2048, 16, 16, 8, 128], P('rcv', None, 'src')
The draws below stay inside these ranges and needn't reach their ends.
Inputs may be any that keep to these rules, and one draw needn't show every extreme that they name: Some window starts at 10180. block_mask[a, b, c] is 0 wherever b < a.
All inputs are finite; a program needn't handle non-finite values.
Results may differ from the reference program's by a relative error of at most 0.0065.
Values may be sent and summed in bfloat16 or wider, within the bound.
No kernel may reach another device: no remote copies, remote signals or barrier semaphores. Data moves between devices by JAX's collectives and lax.ppermute only.
A program may use at most 192 MiB of HBM per device.

```python
import math
import jax
import jax.numpy as jnp
from jax import lax

CH_DEV = 8
WINDOWS = 2
DEC = 5
KSEG = 13
NT = 2048
FB = 512
HALF = 64
LAGS = 128
TAPS = 65
F = 1024
RAW = 10300
REC = 20480
BLOCK = 128
BLOCKS = 16
SUBS = 16
CHANNELS = 2048


def draw_records(key, part):
    key = jax.random.fold_in(key, 5)
    subkeys = jax.random.split(key, 6)
    tone_count = 4
    noise = jnp.clip(jax.random.normal(subkeys[0], (CHANNELS, REC), jnp.float32), -5.0, 5.0)
    channel_gain = jnp.exp(jax.random.uniform(subkeys[1], (CHANNELS, 1), jnp.float32, 0.0, math.log(10.0)))
    tone_bins = jax.random.randint(subkeys[2], (CHANNELS, tone_count), REC // 400, REC // 20)
    offsets = jax.random.randint(subkeys[3], (CHANNELS, tone_count), 0, REC)
    tone_level = jax.random.uniform(subkeys[4], (CHANNELS, tone_count), jnp.float32, 0.5, 2.0)
    drift = jax.random.uniform(subkeys[5], (CHANNELS, 1), jnp.float32, -math.pi, math.pi)
    sample_ids = jnp.arange(REC, dtype=jnp.int32)[None, :]
    signal = noise
    for tone in range(tone_count):
        phase_index = (tone_bins[:, tone:tone + 1] * sample_ids + offsets[:, tone:tone + 1]) % REC
        signal = signal + tone_level[:, tone:tone + 1] * jnp.sin(2.0 * math.pi / REC * phase_index.astype(jnp.float32))
    slow_index = 3 * sample_ids % REC
    envelope = jnp.exp(0.8 * jnp.sin(2.0 * math.pi / REC * slow_index.astype(jnp.float32) + drift))
    return (channel_gain * envelope * signal).astype(jnp.float32)


def draw_starts(key, part):
    key = jax.random.fold_in(key, 7)
    subkeys = jax.random.split(key, 2)
    latest = REC - RAW
    chosen_starts = jax.random.randint(subkeys[0], (WINDOWS,), 0, latest + 1)
    chosen = jax.random.randint(subkeys[1], (), 0, WINDOWS)
    window_ids = jnp.arange(WINDOWS)
    chosen_starts = jnp.where(window_ids == chosen, latest, chosen_starts)
    return chosen_starts.astype(jnp.int32)


def draw_block_mask(key, part):
    key = jax.random.fold_in(key, 11)
    chosen = jax.random.randint(key, (BLOCKS, BLOCKS, SUBS), 0, 4)
    source_ids = jnp.arange(BLOCKS)[:, None, None]
    receiver_ids = jnp.arange(BLOCKS)[None, :, None]
    return jnp.where((receiver_ids >= source_ids) & (chosen > 0), 1, 0).astype(jnp.int32)


def setup_inputs(seed: int = 0) -> dict:
    key_of = jax.random.split(jax.random.key(seed), 4)
    records = draw_records(jax.random.fold_in(key_of[3], 71), 0)
    starts = draw_starts(jax.random.fold_in(key_of[3], 71), 0)
    block_mask = draw_block_mask(jax.random.fold_in(key_of[3], 71), 0)
    return {"records": records, "starts": starts, "block_mask": block_mask}


eps_power = 1e-06

def lowpass():
    tap_index = jnp.arange(TAPS, dtype=jnp.float32)
    centre = (TAPS - 1) / 2.0
    taper = 0.5 - 0.5 * jnp.cos(2.0 * math.pi * (tap_index + 1.0) / (TAPS + 1.0))
    return jnp.sinc((tap_index - centre) / DEC) * taper / DEC

def decimate(windows):
    taps_kernel = lowpass()
    frames = windows.reshape(windows.shape[0], windows.shape[1], NT + KSEG - 1, DEC)
    phases = jnp.swapaxes(frames, 2, 3)
    traces = jnp.zeros((windows.shape[0], windows.shape[1], NT), jnp.float32)
    for segment in range(KSEG):
        weights = taps_kernel[segment * DEC:(segment + 1) * DEC]
        traces = traces + lax.optimization_barrier(jnp.sum(phases[:, :, :, segment:segment + NT] * weights[:, None], axis=2))
    return traces

def smoother(bins, band, reach):
    source_bins = jnp.arange(bins, dtype=jnp.int32)[:, None]
    target_bins = jnp.arange(band, dtype=jnp.int32)[None, :]
    inside = jnp.abs(source_bins - target_bins) <= reach
    lowest = jnp.maximum(target_bins - reach, 0)
    highest = jnp.minimum(target_bins + reach, bins - 1)
    counted = (highest - lowest + 1).astype(jnp.float32)
    return jnp.where(inside, 1.0, 0.0).astype(jnp.float32) / counted

def finish(real_part, imag_part, window_count, channel_count):
    power = real_part * real_part + imag_part * imag_part
    smoothed = jnp.dot(power, smoother(F, FB, HALF), precision=lax.Precision.HIGHEST)
    divisor = jnp.sqrt(smoothed + eps_power)
    whitened = jnp.stack([real_part[:, :FB] / divisor, imag_part[:, :FB] / divisor], axis=1)
    whitened = whitened.reshape(window_count, channel_count, 2, FB)
    return jnp.transpose(whitened, (1, 0, 2, 3)).astype(jnp.bfloat16)

def whiten(records, starts):
    windows = jax.vmap(lambda window_start: lax.dynamic_slice_in_dim(records, window_start, RAW, 1))(starts)
    traces = decimate(windows)
    spectrum = jnp.fft.rfft(traces, axis=-1)[:, :, :F]
    real_part = jnp.real(spectrum).reshape(-1, F)
    imag_part = jnp.imag(spectrum).reshape(-1, F)
    return finish(real_part, imag_part, traces.shape[0], traces.shape[1])

def lag_table(band, lag_count, samples):
    bin_ids = jnp.arange(band, dtype=jnp.int32)[:, None]
    lag_ids = jnp.arange(lag_count, dtype=jnp.int32)[None, :] - lag_count // 2 + samples
    phase_index = bin_ids * lag_ids % samples
    radians = 2.0 * math.pi / samples * phase_index.astype(jnp.float32)
    return jnp.concatenate([jnp.cos(radians), -jnp.sin(radians)], axis=0).astype(jnp.bfloat16)

def correlate(sources, receivers, inverse):
    sources = sources.astype(jnp.float32)
    receivers = receivers.astype(jnp.float32)

    def pair_sum(first_side, second_side):
        return jnp.einsum('iwf,jwf->ijf', first_side, second_side)
    cross_real = pair_sum(sources[:, :, 0], receivers[:, :, 0]) + pair_sum(sources[:, :, 1], receivers[:, :, 1])
    cross_imag = pair_sum(sources[:, :, 1], receivers[:, :, 0]) - pair_sum(sources[:, :, 0], receivers[:, :, 1])
    cross = jnp.concatenate([cross_real, cross_imag], axis=2).astype(jnp.bfloat16)
    cross = cross.reshape(-1, cross.shape[2])
    return jnp.dot(cross, inverse, preferred_element_type=jnp.float32)

def reference(records, starts, block_mask):
    spectra = whiten(records, starts)
    inverse = lag_table(FB, LAGS, NT)
    normalizer = 1.0 / math.sqrt(WINDOWS * FB)
    blocks = spectra.reshape(BLOCKS, BLOCK, WINDOWS, 2, FB)
    local_ids = jnp.arange(BLOCK, dtype=jnp.int32)

    def one_pair(src_block, rcv_block):
        lagged = correlate(blocks[src_block], blocks[rcv_block], inverse).reshape(BLOCK, BLOCK, LAGS) * normalizer
        source_ids = src_block * BLOCK + local_ids
        receiver_ids = rcv_block * BLOCK + local_ids
        allowed = jnp.repeat(block_mask[src_block, rcv_block], CH_DEV)
        keep_pair = (source_ids[:, None] < receiver_ids[None, :]) & (allowed[None, :] > 0)
        return jnp.where(keep_pair[:, :, None], lagged, 0.0).astype(jnp.bfloat16)

    def row_of(src_block):

        def column_of(rcv_block):
            return lax.cond(rcv_block >= src_block, lambda: one_pair(src_block, rcv_block), lambda: jnp.zeros((BLOCK, BLOCK, LAGS), jnp.bfloat16))
        columns = lax.map(column_of, jnp.arange(BLOCKS, dtype=jnp.int32))
        return jnp.transpose(columns, (1, 0, 2, 3))
    rows_all = lax.map(row_of, jnp.arange(BLOCKS, dtype=jnp.int32))
    return rows_all.reshape(CHANNELS, BLOCKS, SUBS, CH_DEV, LAGS)
```

```python
import functools
import math

import jax
import jax.numpy as jnp
import numpy as np
from jax import lax
from jax.experimental import pallas as pl
from jax.experimental.pallas import tpu as pltpu
from jax.sharding import PartitionSpec as P

DEC = 5
NT = 2048
FB = 512
HALF = 64
LAGS = 128
TAPS = 65
F = 1024
RAW = 10300
WINDOWS = 2
BLOCKS = 16
PIECE = 8
GROUP = 16
LANES = 128
FINE = 8
COARSE = LAGS // FINE
EPS = 1e-06
SPEC = WINDOWS * 2 * FB


def lowpass():
    k = np.arange(TAPS, dtype=np.float64)
    taper = 0.5 - 0.5 * np.cos(2.0 * np.pi * (k + 1.0) / (TAPS + 1.0))
    return np.sinc((k - (TAPS - 1) / 2.0) / DEC) * taper / DEC


def decimation_matrix():
    taps = lowpass()
    matrix = np.zeros((6 * LANES, LANES))
    for n in range(LANES):
        matrix[DEC * n : DEC * n + TAPS, n] = taps
    return matrix.astype(np.float32)


def tile_bins():
    bins = -np.ones((8, LANES), np.int64)
    first = np.zeros((8, LANES), np.int64)
    for tile in range(8):
        pair, side = tile // 2, tile % 2
        for half in range(2):
            low = (0, 8)[half] if tile == 0 else (tile, GROUP - tile)[half]
            for high in range((FB + HALF) // GROUP):
                if high < FB // GROUP:
                    column = side * 64 + half * 32 + high
                else:
                    column = (1 - side) * 64 + pair * 8 + half * 4 + high - FB // GROUP
                bins[tile, column] = GROUP * high + low
                first[tile, column] = half
    return bins, first


def fourier_tiles():
    bins, half_of = tile_bins()
    m = np.arange(LANES)
    tiles = np.zeros((8, 2 * LANES, 2 * LANES))
    for tile in range(8):
        for column in range(LANES):
            f = bins[tile, column]
            if f < 0:
                continue
            angle = 2.0 * np.pi * ((f * m) % NT) / NT
            c, s = np.cos(angle), np.sin(angle)
            half = half_of[tile, column]
            if tile == 0:
                rows = slice(half * LANES, (half + 1) * LANES)
                tiles[tile, rows, column] = c
                tiles[tile, rows, LANES + column] = -s
            else:
                sign = 1.0 if half == 0 else -1.0
                tiles[tile, :LANES, column] = c
                tiles[tile, LANES:, column] = sign * s
                tiles[tile, :LANES, LANES + column] = -s
                tiles[tile, LANES:, LANES + column] = sign * c
    return tiles.astype(np.float32)


def band_bins():
    bins, _ = tile_bins()
    band = []
    extra = -np.ones(LANES, np.int64)
    for pair in range(4):
        left, right = bins[2 * pair], bins[2 * pair + 1]
        band.append(np.where(np.arange(LANES) < 64, left, right))
        swapped = np.where(np.arange(LANES) < 64, right, left)
        extra = np.where(swapped >= 0, swapped, extra)
    return np.concatenate(band), extra


def smoother():
    band, extra = band_bins()
    source = np.concatenate([band, extra])[:, None]
    target = band[None, :]
    inside = (np.abs(source - target) <= HALF) & (source >= 0)
    counted = np.minimum(band + HALF, F - 1) - np.maximum(band - HALF, 0) + 1
    return inside.astype(np.float32), (1.0 / counted).astype(np.float32)[None, :]


def phases(lags, scale):
    band, _ = band_bins()
    angle = 2.0 * np.pi * ((lags[:, None] * band[None, :]) % NT) / NT
    return np.stack([np.cos(angle), np.sin(angle)]).astype(np.float32) * np.float32(scale)


def plus(a, b):
    if a is None:
        return b
    return a if b is None else a + b


def minus(a, b):
    if b is None:
        return a
    return -b if a is None else a - b


def times(a, factor):
    return None if a is None or factor == 0.0 else (a if factor == 1.0 else (-a if factor == -1.0 else a * factor))


def small_fourier(values):
    count = len(values)
    if count == 1:
        return values
    even, odd = small_fourier(values[0::2]), small_fourier(values[1::2])
    low, high = [], []
    for f in range(count // 2):
        angle = 2.0 * math.pi * f / count
        c, s = math.cos(angle), math.sin(angle)
        c = 0.0 if 4 * f == count else c
        real, imag = odd[f]
        turned = (plus(times(real, c), times(imag, s)), minus(times(imag, c), times(real, s)))
        low.append((plus(even[f][0], turned[0]), plus(even[f][1], turned[1])))
        high.append((minus(even[f][0], turned[0]), minus(even[f][1], turned[1])))
    return low + high


def whiten_kernel(starts, records, decimate, fourier, smooth, inverse_count, out, raw):
    lane = lax.broadcasted_iota(jnp.int32, (PIECE, LANES), 1)
    used = 5 * GROUP + 1
    last_tile = records.shape[1] // LANES - 1
    for w in range(WINDOWS):
        start = starts[w]
        base = start // LANES
        offset = start % LANES
        turn = (LANES - offset) % LANES
        own = lane < LANES - offset

        def turned(v):
            at = jnp.minimum(base + v, last_tile)
            return pltpu.roll(records[:, pl.ds(pl.multiple_of(at * LANES, LANES), LANES)], turn, 1)

        now = turned(0)
        for v in range(used):
            later = turned(v + 1)
            moved = jnp.where(own, now, later)
            now = later
            run, part = v // 5, v % 5
            if run < GROUP:
                raw[run * 16 + w * 8 : run * 16 + w * 8 + 8, part * LANES : (part + 1) * LANES] = moved
            if part == 0 and run > 0:
                raw[(run - 1) * 16 + w * 8 : (run - 1) * 16 + w * 8 + 8, 5 * LANES :] = moved
    traces = jnp.dot(raw[...], decimate[...], precision=lax.Precision.HIGHEST, preferred_element_type=jnp.float32)
    parts = small_fourier([(traces[16 * run : 16 * run + 16], None) for run in range(GROUP)])
    left = lax.broadcasted_iota(jnp.int32, (16, LANES), 1) < 64
    real_tiles, imag_tiles = [], []
    for tile in range(8):
        if tile == 0:
            pair = [parts[0][0], parts[8][0]]
        else:
            pair = list(parts[tile])
        both = jnp.dot(
            jnp.concatenate(pair, axis=1), fourier[tile], precision=lax.Precision.HIGHEST,
            preferred_element_type=jnp.float32,
        )
        real_tiles.append(both[:, :LANES])
        imag_tiles.append(both[:, LANES:])
    reals, imags, powers = [], [], []
    extra = None
    for pair in range(4):
        ra, rb = real_tiles[2 * pair], real_tiles[2 * pair + 1]
        ia, ib = imag_tiles[2 * pair], imag_tiles[2 * pair + 1]
        reals.append(jnp.where(left, ra, rb))
        imags.append(jnp.where(left, ia, ib))
        pa, pb = ra * ra + ia * ia, rb * rb + ib * ib
        powers.append(jnp.where(left, pa, pb))
        extra = plus(extra, jnp.where(left, pb, pa))
    power = jnp.concatenate(powers + [extra], axis=1)
    first = power.astype(jnp.bfloat16)
    rest = power - first.astype(jnp.float32)
    second = rest.astype(jnp.bfloat16)
    third = (rest - second.astype(jnp.float32)).astype(jnp.bfloat16)
    sums = jnp.dot(
        jnp.concatenate([first, second, third], axis=0), smooth[...], preferred_element_type=jnp.float32
    )
    smoothed = (sums[:16] + sums[16:32] + sums[32:]) * inverse_count[...]
    gain = lax.rsqrt(smoothed + EPS)
    for q, values in enumerate((reals, imags)):
        white = (jnp.concatenate(values, axis=1) * gain).astype(jnp.bfloat16)
        for w in range(WINDOWS):
            out[:, (2 * w + q) * FB : (2 * w + q + 1) * FB] = white[8 * w : 8 * w + 8]


def whiten(records, starts):
    decimate = decimation_matrix()
    fourier = fourier_tiles()
    smooth, inverse_count = smoother()
    vmem = pl.BlockSpec(memory_space=pltpu.VMEM)
    return pl.pallas_call(
        whiten_kernel,
        out_shape=jax.ShapeDtypeStruct((PIECE, SPEC), jnp.bfloat16),
        in_specs=[pl.BlockSpec(memory_space=pltpu.SMEM)] + [vmem] * 5,
        out_specs=vmem,
        scratch_shapes=[pltpu.VMEM((16 * GROUP, 6 * LANES), jnp.float32)],
        compiler_params=pltpu.CompilerParams(vmem_limit_bytes=32 * 1024 * 1024),
    )(
        starts, records, jnp.asarray(decimate), jnp.asarray(fourier),
        jnp.asarray(smooth).astype(jnp.bfloat16), jnp.asarray(inverse_count),
    )


def swap_groups(values):
    lane_group = lax.broadcasted_iota(jnp.int32, values[0].shape, 1) // FINE
    values = list(values)
    for bit in (3, 2, 1, 0):
        distance = 1 << bit
        low_half = (lane_group & distance) == 0
        for a in range(COARSE):
            if a & distance:
                continue
            low, high = values[a], values[a + distance]
            shift = distance * FINE
            values[a] = jnp.where(low_half, low, pltpu.roll(high, shift, 1))
            values[a + distance] = jnp.where(low_half, pltpu.roll(low, LANES - shift, 1), high)
    return values


def correlate_kernel(places, limits, order, mine, other, receivers, fine, coarse, out, turned, spread, sources):
    step = pl.program_id(0)

    @pl.when(step == 0)
    def _():
        for side, rows in enumerate((mine, other)):

            @pl.loop(0, 8)
            def _(piece):
                at = pl.multiple_of(places[side * 8 + piece] * PIECE, PIECE)
                values = rows[piece].astype(jnp.float32)
                sources[...] = values
                for pair in range(PIECE // 2):
                    for w in range(WINDOWS):
                        at_w = 2 * w * FB
                        reals, imags = [], []
                        for k in range(2):
                            ch = 2 * pair + k
                            real = jnp.broadcast_to(sources[ch : ch + 1, at_w : at_w + FB], (FINE, FB))
                            imag = jnp.broadcast_to(sources[ch : ch + 1, at_w + FB : at_w + 2 * FB], (FINE, FB))
                            c, s = fine[0], fine[1]
                            reals.append(real * c - imag * s)
                            imags.append(real * s + imag * c)
                        target = pl.ds(pl.multiple_of(at * FINE + pair * 16, 16), 16)
                        turned[target, at_w : at_w + FB] = jnp.concatenate(reals, 0).astype(jnp.bfloat16)
                        turned[target, at_w + FB : at_w + 2 * FB] = jnp.concatenate(imags, 0).astype(jnp.bfloat16)

    for piece in range(2):
        held = receivers[0, piece].astype(jnp.float32)
        for w in range(WINDOWS):
            at_w = 2 * w * FB
            real, imag = held[:, at_w : at_w + FB], held[:, at_w + FB : at_w + 2 * FB]
            for pair in range(COARSE // 2):
                reals, imags = [], []
                for k in range(2):
                    lag = 2 * pair + k
                    c = jnp.broadcast_to(coarse[0, lag : lag + 1], (PIECE, FB))
                    s = jnp.broadcast_to(coarse[1, lag : lag + 1], (PIECE, FB))
                    reals.append(real * c - imag * s)
                    imags.append(real * s + imag * c)
                row = piece * COARSE * PIECE + pair * 16
                spread[row : row + 16, at_w : at_w + FB] = jnp.concatenate(reals, 0).astype(jnp.bfloat16)
                spread[row : row + 16, at_w + FB : at_w + 2 * FB] = jnp.concatenate(imags, 0).astype(jnp.bfloat16)

    sublane = lax.broadcasted_iota(jnp.int32, (PIECE, LANES), 0)
    for chunk in range(4):
        lagged = lax.dot_general(
            spread[...], turned[chunk * 256 : (chunk + 1) * 256, :], (((1,), (1,)), ((), ())),
            preferred_element_type=jnp.float32,
        )
        for piece in range(2):
            limit = sublane + limits[2 * order[step] + piece]
            for half in range(2):
                rows = piece * COARSE * PIECE
                values = [
                    lagged[rows + lag * PIECE : rows + (lag + 1) * PIECE, half * LANES : (half + 1) * LANES]
                    for lag in range(COARSE)
                ]
                for k, value in enumerate(swap_groups(values)):
                    source = chunk * 32 + half * 16 + k
                    out[source, piece] = jnp.where(limit > source, value, 0.0).astype(jnp.bfloat16)


def correlate(places, limits, order, mine, other, receivers):
    fine = phases(np.arange(FINE), 1.0)
    coarse = phases(-(FINE * np.arange(COARSE) - LAGS // 2), 1.0 / math.sqrt(WINDOWS * FB))
    whole = lambda *shape: pl.BlockSpec(shape, lambda i, *_: (0,) * len(shape))
    grid_spec = pltpu.PrefetchScalarGridSpec(
        num_scalar_prefetch=3,
        grid=(8,),
        in_specs=[
            whole(8, PIECE, SPEC), whole(8, PIECE, SPEC),
            pl.BlockSpec((1, 2, PIECE, SPEC), lambda i, *_: (i, 0, 0, 0)),
            whole(2, FINE, FB), whole(2, COARSE, FB),
        ],
        out_specs=pl.BlockSpec((128, 2, PIECE, LAGS), lambda i, places, limits, order: (0, order[i], 0, 0)),
        scratch_shapes=[
            pltpu.VMEM((128 * FINE, SPEC), jnp.bfloat16),
            pltpu.VMEM((2 * COARSE * PIECE, SPEC), jnp.bfloat16),
            pltpu.VMEM((PIECE, SPEC), jnp.float32),
        ],
    )
    return pl.pallas_call(
        correlate_kernel,
        grid_spec=grid_spec,
        out_shape=jax.ShapeDtypeStruct((128, BLOCKS, PIECE, LAGS), jnp.bfloat16),
        compiler_params=pltpu.CompilerParams(vmem_limit_bytes=40 * 1024 * 1024),
    )(places, limits, order, mine, other, receivers, jnp.asarray(fine), jnp.asarray(coarse))


def move(block, axis, source_of):
    return lax.ppermute(block, axis, [(source_of(i), i) for i in range(lax.axis_size(axis))])


def on_device(records, starts, block_mask):
    own = whiten(records, starts)
    src = lax.axis_index("src")
    rcv = lax.axis_index("rcv")
    x, y_lo, core = src // 4, (src // 2) % 2, src % 2
    z, y_hi = rcv // 2, rcv % 2

    near = move(own, "src", lambda i: i ^ 2)
    two = jnp.where(y_lo == 0, jnp.stack([own, near]), jnp.stack([near, own]))
    mine = [two] + [
        move(two, "src", lambda i, k=k: ((i // 4 + k) % 4) * 4 + i % 4) for k in (1, 2, 3)
    ]
    mine = jnp.concatenate(mine, axis=0)
    other = move(mine, "src", lambda i: i ^ 1)

    far = move(own, "rcv", lambda i: i ^ 1)
    pair = jnp.where(y_hi == 0, jnp.stack([own, far]), jnp.stack([far, own]))
    pairs = [pair] + [
        move(pair, "rcv", lambda i, k=k: ((i // 2 + k) % 8) * 2 + i % 2) for k in range(1, 8)
    ]
    receivers = jnp.stack(pairs)

    k = jnp.arange(8, dtype=jnp.int32)
    chip = ((x + k // 2) % 4) * 4 + (k % 2) * 2
    places = jnp.concatenate([chip + core, chip + 1 - core])
    order = (z + k) % 8
    pieces = jnp.arange(BLOCKS, dtype=jnp.int32)
    wanted = block_mask.reshape(-1) > 0
    limits = jnp.where(
        wanted & (pieces >= rcv), jnp.where(pieces == rcv, src * PIECE, 4096), -4096
    ).astype(jnp.int32)
    result = correlate(places, limits, order, mine, other, receivers)
    return result.reshape(128, BLOCKS, 1, PIECE, LAGS)


def solution(mesh):
    in_specs = (P(("rcv", "src"), None), P(), P("rcv", None, "src"))
    out_specs = P("rcv", None, "src", None, None)
    return jax.shard_map(
        on_device, mesh=mesh, in_specs=in_specs, out_specs=out_specs, check_vma=False
    )
```

```python
import functools
import math

import jax
import jax.numpy as jnp
import numpy as np
from jax import lax
from jax.experimental import pallas as pl
from jax.experimental.pallas import tpu as pltpu
from jax.sharding import PartitionSpec as P

DEC = 5
NT = 2048
FB = 512
HALF = 64
LAGS = 128
TAPS = 65
F = 1024
RAW = 10300
WINDOWS = 2
BLOCKS = 16
PIECE = 8
GROUP = 16
LANES = 128
FINE = 8
COARSE = LAGS // FINE
EPS = 1e-06
SPEC = WINDOWS * 2 * FB


def lowpass():
    k = np.arange(TAPS, dtype=np.float64)
    taper = 0.5 - 0.5 * np.cos(2.0 * np.pi * (k + 1.0) / (TAPS + 1.0))
    return np.sinc((k - (TAPS - 1) / 2.0) / DEC) * taper / DEC


def decimation_matrix():
    taps = lowpass()
    matrix = np.zeros((6 * LANES, LANES))
    for n in range(LANES):
        matrix[DEC * n : DEC * n + TAPS, n] = taps
    return matrix.astype(np.float32)


def tile_bins():
    bins = -np.ones((8, LANES), np.int64)
    first = np.zeros((8, LANES), np.int64)
    for tile in range(8):
        pair, side = tile // 2, tile % 2
        for half in range(2):
            low = (0, 8)[half] if tile == 0 else (tile, GROUP - tile)[half]
            for high in range((FB + HALF) // GROUP):
                if high < FB // GROUP:
                    column = side * 64 + half * 32 + high
                else:
                    column = (1 - side) * 64 + pair * 8 + half * 4 + high - FB // GROUP
                bins[tile, column] = GROUP * high + low
                first[tile, column] = half
    return bins, first


def fourier_tiles():
    bins, half_of = tile_bins()
    m = np.arange(LANES)
    tiles = np.zeros((8, 2 * LANES, 2 * LANES))
    for tile in range(8):
        for column in range(LANES):
            f = bins[tile, column]
            if f < 0:
                continue
            angle = 2.0 * np.pi * ((f * m) % NT) / NT
            c, s = np.cos(angle), np.sin(angle)
            half = half_of[tile, column]
            if tile == 0:
                rows = slice(half * LANES, (half + 1) * LANES)
                tiles[tile, rows, column] = c
                tiles[tile, rows, LANES + column] = -s
            else:
                sign = 1.0 if half == 0 else -1.0
                tiles[tile, :LANES, column] = c
                tiles[tile, LANES:, column] = sign * s
                tiles[tile, :LANES, LANES + column] = -s
                tiles[tile, LANES:, LANES + column] = sign * c
    return tiles.astype(np.float32)


def band_bins():
    bins, _ = tile_bins()
    band = []
    extra = -np.ones(LANES, np.int64)
    for pair in range(4):
        left, right = bins[2 * pair], bins[2 * pair + 1]
        band.append(np.where(np.arange(LANES) < 64, left, right))
        swapped = np.where(np.arange(LANES) < 64, right, left)
        extra = np.where(swapped >= 0, swapped, extra)
    return np.concatenate(band), extra


def smoother():
    band, _ = band_bins()
    counted = np.minimum(band + HALF, F - 1) - np.maximum(band - HALF, 0) + 1
    return np.stack([band.astype(np.float32), (1.0 / counted).astype(np.float32)])


def phases(lags, scale):
    band, _ = band_bins()
    angle = 2.0 * np.pi * ((lags[:, None] * band[None, :]) % NT) / NT
    return np.stack([np.cos(angle), np.sin(angle)]).astype(np.float32) * np.float32(scale)


def plus(a, b):
    if a is None:
        return b
    return a if b is None else a + b


def minus(a, b):
    if b is None:
        return a
    return -b if a is None else a - b


def times(a, factor):
    return None if a is None or factor == 0.0 else (a if factor == 1.0 else (-a if factor == -1.0 else a * factor))


def small_fourier(values):
    count = len(values)
    if count == 1:
        return values
    even, odd = small_fourier(values[0::2]), small_fourier(values[1::2])
    low, high = [], []
    for f in range(count // 2):
        angle = 2.0 * math.pi * f / count
        c, s = math.cos(angle), math.sin(angle)
        c = 0.0 if 4 * f == count else c
        real, imag = odd[f]
        turned = (plus(times(real, c), times(imag, s)), minus(times(imag, c), times(real, s)))
        low.append((plus(even[f][0], turned[0]), plus(even[f][1], turned[1])))
        high.append((minus(even[f][0], turned[0]), minus(even[f][1], turned[1])))
    return low + high


def source_bins():
    row = lax.broadcasted_iota(jnp.int32, (5 * LANES, LANES), 0)
    within = row % LANES
    is_band = row < FB
    side = jnp.where(is_band, within // 64, 1 - within // 64)
    pair = jnp.where(is_band, row // LANES, within % 64 // 8)
    half = jnp.where(is_band, within % 64 // 32, within % 8 // 4)
    high = jnp.where(is_band, within % 32, FB // GROUP + within % 4)
    tile = 2 * pair + side
    low = jnp.where(half == 0, tile, jnp.where(tile == 0, GROUP // 2, GROUP - tile))
    used = is_band | (within % 64 < 32)
    return jnp.where(used, GROUP * high + low, -1000).astype(jnp.float32)


def whiten_kernel(
    starts_hbm, records_hbm, decimate_hbm, fourier_hbm, smooth_hbm, out,
    starts, records, decimate, fourier, smooth, raw, done,
):
    pairs = [
        (starts_hbm, starts), (records_hbm, records), (decimate_hbm, decimate),
        (fourier_hbm, fourier), (smooth_hbm, smooth),
    ]
    copies = [pltpu.make_async_copy(a, b, done.at[n]) for n, (a, b) in enumerate(pairs)]
    for copy in copies:
        copy.start()
    copies[0].wait()
    copies[1].wait()
    lane = lax.broadcasted_iota(jnp.int32, (PIECE, LANES), 1)
    used = 5 * GROUP + 1
    last_tile = records.shape[1] // LANES - 1
    for w in range(WINDOWS):
        start = starts[w]
        base = start // LANES
        offset = start % LANES
        turn = (LANES - offset) % LANES
        own = lane < LANES - offset

        def turned(v):
            at = jnp.minimum(base + v, last_tile)
            return pltpu.roll(records[:, pl.ds(pl.multiple_of(at * LANES, LANES), LANES)], turn, 1)

        now = turned(0)
        for v in range(used):
            later = turned(v + 1)
            moved = jnp.where(own, now, later)
            now = later
            run, part = v // 5, v % 5
            if run < GROUP:
                raw[run * 16 + w * 8 : run * 16 + w * 8 + 8, part * LANES : (part + 1) * LANES] = moved
            if part == 0 and run > 0:
                raw[(run - 1) * 16 + w * 8 : (run - 1) * 16 + w * 8 + 8, 5 * LANES :] = moved
    copies[2].wait()
    traces = jnp.dot(raw[...], decimate[...], precision=lax.Precision.HIGHEST, preferred_element_type=jnp.float32)
    parts = small_fourier([(traces[16 * run : 16 * run + 16], None) for run in range(GROUP)])
    left = lax.broadcasted_iota(jnp.int32, (16, LANES), 1) < 64
    copies[3].wait()
    real_tiles, imag_tiles = [], []
    for tile in range(8):
        if tile == 0:
            pair = [parts[0][0], parts[8][0]]
        else:
            pair = list(parts[tile])
        both = jnp.dot(
            jnp.concatenate(pair, axis=1), fourier[tile], precision=lax.Precision.HIGHEST,
            preferred_element_type=jnp.float32,
        )
        real_tiles.append(both[:, :LANES])
        imag_tiles.append(both[:, LANES:])
    reals, imags, powers = [], [], []
    extra = None
    for pair in range(4):
        ra, rb = real_tiles[2 * pair], real_tiles[2 * pair + 1]
        ia, ib = imag_tiles[2 * pair], imag_tiles[2 * pair + 1]
        reals.append(jnp.where(left, ra, rb))
        imags.append(jnp.where(left, ia, ib))
        pa, pb = ra * ra + ia * ia, rb * rb + ib * ib
        powers.append(jnp.where(left, pa, pb))
        extra = plus(extra, jnp.where(left, pb, pa))
    power = jnp.concatenate(powers + [extra], axis=1)
    first = power.astype(jnp.bfloat16)
    rest = power - first.astype(jnp.float32)
    second = rest.astype(jnp.bfloat16)
    third = (rest - second.astype(jnp.float32)).astype(jnp.bfloat16)
    copies[4].wait()
    bins = source_bins()
    window = jnp.concatenate(
        [
            jnp.where(jnp.abs(bins - smooth[0:1, q * LANES : (q + 1) * LANES]) <= HALF, 1.0, 0.0).astype(jnp.bfloat16)
            for q in range(4)
        ],
        axis=1,
    )
    sums = jnp.dot(
        jnp.concatenate([first, second, third], axis=0), window, preferred_element_type=jnp.float32
    )
    smoothed = (sums[:16] + sums[16:32] + sums[32:]) * smooth[1:2, :]
    gain = lax.rsqrt(smoothed + EPS)
    for q, values in enumerate((reals, imags)):
        white = (jnp.concatenate(values, axis=1) * gain).astype(jnp.bfloat16)
        for w in range(WINDOWS):
            for copy in range(8):
                out[copy, :, (2 * w + q) * FB : (2 * w + q + 1) * FB] = white[8 * w : 8 * w + 8]


def whiten(records, starts):
    decimate = decimation_matrix()
    fourier = fourier_tiles()
    smooth = smoother()
    vmem = pl.BlockSpec(memory_space=pltpu.VMEM)
    hbm = pl.BlockSpec(memory_space=pltpu.HBM)
    return pl.pallas_call(
        whiten_kernel,
        out_shape=jax.ShapeDtypeStruct((8, PIECE, SPEC), jnp.bfloat16),
        in_specs=[hbm] * 5,
        out_specs=vmem,
        scratch_shapes=[
            pltpu.SMEM((WINDOWS,), jnp.int32),
            pltpu.VMEM(records.shape, jnp.float32),
            pltpu.VMEM(decimate.shape, jnp.float32),
            pltpu.VMEM(fourier.shape, jnp.float32),
            pltpu.VMEM(smooth.shape, jnp.float32),
            pltpu.VMEM((16 * GROUP, 6 * LANES), jnp.float32),
            pltpu.SemaphoreType.DMA((5,)),
        ],
        compiler_params=pltpu.CompilerParams(vmem_limit_bytes=64 * 1024 * 1024 - 512 * 1024),
    )(
        starts, records, jnp.asarray(decimate), jnp.asarray(fourier), jnp.asarray(smooth),
    )


def swap_groups(values):
    lane_group = lax.broadcasted_iota(jnp.int32, values[0].shape, 1) // FINE
    values = list(values)
    for bit in (3, 2, 1, 0):
        distance = 1 << bit
        low_half = (lane_group & distance) == 0
        for a in range(COARSE):
            if a & distance:
                continue
            low, high = values[a], values[a + distance]
            shift = distance * FINE
            values[a] = jnp.where(low_half, low, pltpu.roll(high, shift, 1))
            values[a + distance] = jnp.where(low_half, pltpu.roll(low, LANES - shift, 1), high)
    return values


def turn_kernel(own, other, fine, turned, sources):
    core = lax.axis_index("src") % 2
    for side, rows in enumerate((own, other)):

        @pl.loop(0, 8)
        def _(piece):
            place = 2 * piece + (core if side == 0 else 1 - core)
            sources[...] = rows[piece].astype(jnp.float32)
            for pair in range(PIECE // 2):
                for w in range(WINDOWS):
                    at_w = 2 * w * FB
                    reals, imags = [], []
                    for k in range(2):
                        ch = 2 * pair + k
                        real = jnp.broadcast_to(sources[ch : ch + 1, at_w : at_w + FB], (FINE, FB))
                        imag = jnp.broadcast_to(sources[ch : ch + 1, at_w + FB : at_w + 2 * FB], (FINE, FB))
                        c, s = fine[0], fine[1]
                        reals.append(real * c - imag * s)
                        imags.append(real * s + imag * c)
                    target = pl.ds(pl.multiple_of(place * PIECE * FINE + pair * 16, 16), 16)
                    turned[target, at_w : at_w + FB] = jnp.concatenate(reals, 0).astype(jnp.bfloat16)
                    turned[target, at_w + FB : at_w + 2 * FB] = jnp.concatenate(imags, 0).astype(jnp.bfloat16)


def turn(own, other):
    fine = phases(np.arange(FINE), 1.0)
    vmem = pl.BlockSpec(memory_space=pltpu.VMEM)
    return pl.pallas_call(
        turn_kernel,
        out_shape=jax.ShapeDtypeStruct((128 * FINE, SPEC), jnp.bfloat16),
        in_specs=[vmem] * 3,
        out_specs=vmem,
        scratch_shapes=[pltpu.VMEM((PIECE, SPEC), jnp.float32)],
        cost_estimate=pl.CostEstimate(flops=6 * 128 * FINE * SPEC, bytes_accessed=5 << 20, transcendentals=0),
        compiler_params=pltpu.CompilerParams(vmem_limit_bytes=16 * 1024 * 1024),
    )(own, other, jnp.asarray(fine))


PER = 4


def correlate_kernel(flip, mask, receivers, turned, coarse, *rest):
    out, spread = rest[-2:]
    step = pl.program_id(0)
    src, rcv = lax.axis_index("src"), lax.axis_index("rcv")
    y_hi = (rcv + flip) % 2
    for piece in range(PER):
        held = receivers[piece].astype(jnp.float32)
        for w in range(WINDOWS):
            at_w = 2 * w * FB
            real, imag = held[:, at_w : at_w + FB], held[:, at_w + FB : at_w + 2 * FB]
            for pair in range(COARSE // 2):
                reals, imags = [], []
                for k in range(2):
                    lag = 2 * pair + k
                    c = jnp.broadcast_to(coarse[0, lag : lag + 1], (PIECE, FB))
                    s = jnp.broadcast_to(coarse[1, lag : lag + 1], (PIECE, FB))
                    reals.append(real * c - imag * s)
                    imags.append(real * s + imag * c)
                row = piece * COARSE * PIECE + pair * 16
                spread[row : row + 16, at_w : at_w + FB] = jnp.concatenate(reals, 0).astype(jnp.bfloat16)
                spread[row : row + 16, at_w + FB : at_w + 2 * FB] = jnp.concatenate(imags, 0).astype(jnp.bfloat16)

    sublane = lax.broadcasted_iota(jnp.int32, (PIECE, LANES), 0)
    limits = []
    for piece in range(PER):
        block = 2 * (PER * step + piece) + y_hi
        limit = jnp.where(block == rcv, src * PIECE, 4096)
        limits.append(sublane + jnp.where((block >= rcv) & (mask[block] > 0), limit, -4096))
    for chunk in range(4):
        lagged = lax.dot_general(
            spread[...], turned[chunk * 256 : (chunk + 1) * 256, :], (((1,), (1,)), ((), ())),
            preferred_element_type=jnp.float32,
        )
        for piece in range(PER):
            for half in range(2):
                rows = piece * COARSE * PIECE
                values = [
                    lagged[rows + lag * PIECE : rows + (lag + 1) * PIECE, half * LANES : (half + 1) * LANES]
                    for lag in range(COARSE)
                ]
                for k, value in enumerate(swap_groups(values)):
                    source = chunk * 32 + half * 16 + k
                    out[source, piece, 0] = jnp.where(limits[piece] > source, value, 0.0).astype(jnp.bfloat16)


def correlate(mask, receivers, turned, flip, result=None):
    coarse = phases(-(FINE * np.arange(COARSE) - LAGS // 2), 1.0 / math.sqrt(WINDOWS * FB))
    vmem = pl.BlockSpec(memory_space=pltpu.VMEM)
    operands = [mask, receivers, turned, jnp.asarray(coarse)]
    in_specs = [
        pl.BlockSpec(memory_space=pltpu.SMEM),
        pl.BlockSpec((PER, PIECE, SPEC), lambda i: (i, 0, 0)),
        vmem, vmem,
    ]
    aliases = {}
    if result is not None:
        operands.append(result)
        in_specs.append(pl.BlockSpec(memory_space=pltpu.HBM))
        aliases = {4: 0}

    def place(i):
        return 0, i, (lax.axis_index("rcv") + flip) % 2, 0, 0

    return pl.pallas_call(
        functools.partial(correlate_kernel, flip),
        grid=(8 // PER,),
        in_specs=in_specs,
        out_specs=pl.BlockSpec((128, PER, 1, PIECE, LAGS), place),
        out_shape=jax.ShapeDtypeStruct((128, 8, 2, PIECE, LAGS), jnp.bfloat16),
        scratch_shapes=[pltpu.VMEM((PER * COARSE * PIECE, SPEC), jnp.bfloat16)],
        input_output_aliases=aliases,
        cost_estimate=pl.CostEstimate(
            flops=2 * 1024 * 1024 * SPEC, bytes_accessed=6 << 20, transcendentals=0
        ),
        compiler_params=pltpu.CompilerParams(vmem_limit_bytes=24 * 1024 * 1024),
    )(*operands)


def move(block, axis, source_of):
    return lax.ppermute(block, axis, [(source_of(i), i) for i in range(lax.axis_size(axis))])


def on_device(records, starts, block_mask):
    own = whiten(records, starts)
    chips = [[core + 2 * k for k in range(8)] for core in range(2)]
    receivers = lax.all_to_all(own, "rcv", 0, 0, axis_index_groups=chips)
    mine = lax.all_to_all(own, "src", 0, 0, axis_index_groups=chips)
    other = move(mine, "src", lambda i: i ^ 1)
    turned = turn(mine, other)
    far = move(receivers, "rcv", lambda i: i ^ 1)
    mask = block_mask.reshape(-1)
    result = correlate(mask, receivers, turned, 0)
    result = correlate(mask, far, turned, 1, result)
    return result.reshape(128, BLOCKS, 1, PIECE, LAGS)


def solution(mesh):
    in_specs = (P(("rcv", "src"), None), P(), P("rcv", None, "src"))
    out_specs = P("rcv", None, "src", None, None)
    return jax.shard_map(
        on_device, mesh=mesh, in_specs=in_specs, out_specs=out_specs, check_vma=False
    )
```

```python
import functools
import math

import jax
import jax.numpy as jnp
import numpy as np
from jax import lax
from jax.experimental import pallas as pl
from jax.experimental.pallas import tpu as pltpu
from jax.sharding import PartitionSpec as P

DEC = 5
NT = 2048
FB = 512
HALF = 64
LAGS = 128
TAPS = 65
F = 1024
RAW = 10300
WINDOWS = 2
BLOCKS = 16
PIECE = 8
GROUP = 16
LANES = 128
FINE = 8
COARSE = LAGS // FINE
EPS = 1e-06
SPEC = WINDOWS * 2 * FB


def lowpass():
    k = np.arange(TAPS, dtype=np.float64)
    taper = 0.5 - 0.5 * np.cos(2.0 * np.pi * (k + 1.0) / (TAPS + 1.0))
    return np.sinc((k - (TAPS - 1) / 2.0) / DEC) * taper / DEC


def decimation_matrix():
    taps = lowpass()
    matrix = np.zeros((6 * LANES, LANES))
    for n in range(LANES):
        matrix[DEC * n : DEC * n + TAPS, n] = taps
    return matrix.astype(np.float32)


def tile_bins():
    bins = -np.ones((8, LANES), np.int64)
    first = np.zeros((8, LANES), np.int64)
    for tile in range(8):
        pair, side = tile // 2, tile % 2
        for half in range(2):
            low = (0, 8)[half] if tile == 0 else (tile, GROUP - tile)[half]
            for high in range((FB + HALF) // GROUP):
                if high < FB // GROUP:
                    column = side * 64 + half * 32 + high
                else:
                    column = (1 - side) * 64 + pair * 8 + half * 4 + high - FB // GROUP
                bins[tile, column] = GROUP * high + low
                first[tile, column] = half
    return bins, first


def fourier_tiles():
    bins, half_of = tile_bins()
    m = np.arange(LANES)
    tiles = np.zeros((8, 2 * LANES, 2 * LANES))
    for tile in range(8):
        for column in range(LANES):
            f = bins[tile, column]
            if f < 0:
                continue
            angle = 2.0 * np.pi * ((f * m) % NT) / NT
            c, s = np.cos(angle), np.sin(angle)
            half = half_of[tile, column]
            if tile == 0:
                rows = slice(half * LANES, (half + 1) * LANES)
                tiles[tile, rows, column] = c
                tiles[tile, rows, LANES + column] = -s
            else:
                sign = 1.0 if half == 0 else -1.0
                tiles[tile, :LANES, column] = c
                tiles[tile, LANES:, column] = sign * s
                tiles[tile, :LANES, LANES + column] = -s
                tiles[tile, LANES:, LANES + column] = sign * c
    return tiles.astype(np.float32)


def band_bins():
    bins, _ = tile_bins()
    band = []
    extra = -np.ones(LANES, np.int64)
    for pair in range(4):
        left, right = bins[2 * pair], bins[2 * pair + 1]
        band.append(np.where(np.arange(LANES) < 64, left, right))
        swapped = np.where(np.arange(LANES) < 64, right, left)
        extra = np.where(swapped >= 0, swapped, extra)
    return np.concatenate(band), extra


def smoother():
    band, _ = band_bins()
    counted = np.minimum(band + HALF, F - 1) - np.maximum(band - HALF, 0) + 1
    return np.stack([band.astype(np.float32), (1.0 / counted).astype(np.float32)])


def phases(lags, scale):
    band, _ = band_bins()
    angle = 2.0 * np.pi * ((lags[:, None] * band[None, :]) % NT) / NT
    return np.stack([np.cos(angle), np.sin(angle)]).astype(np.float32) * np.float32(scale)


def plus(a, b):
    if a is None:
        return b
    return a if b is None else a + b


def minus(a, b):
    if b is None:
        return a
    return -b if a is None else a - b


def times(a, factor):
    return None if a is None or factor == 0.0 else (a if factor == 1.0 else (-a if factor == -1.0 else a * factor))


def small_fourier(values):
    count = len(values)
    if count == 1:
        return values
    even, odd = small_fourier(values[0::2]), small_fourier(values[1::2])
    low, high = [], []
    for f in range(count // 2):
        angle = 2.0 * math.pi * f / count
        c, s = math.cos(angle), math.sin(angle)
        c = 0.0 if 4 * f == count else c
        real, imag = odd[f]
        turned = (plus(times(real, c), times(imag, s)), minus(times(imag, c), times(real, s)))
        low.append((plus(even[f][0], turned[0]), plus(even[f][1], turned[1])))
        high.append((minus(even[f][0], turned[0]), minus(even[f][1], turned[1])))
    return low + high


def source_bins():
    row = lax.broadcasted_iota(jnp.int32, (5 * LANES, LANES), 0)
    within = row % LANES
    is_band = row < FB
    side = jnp.where(is_band, within // 64, 1 - within // 64)
    pair = jnp.where(is_band, row // LANES, within % 64 // 8)
    half = jnp.where(is_band, within % 64 // 32, within % 8 // 4)
    high = jnp.where(is_band, within % 32, FB // GROUP + within % 4)
    tile = 2 * pair + side
    low = jnp.where(half == 0, tile, jnp.where(tile == 0, GROUP // 2, GROUP - tile))
    used = is_band | (within % 64 < 32)
    return jnp.where(used, GROUP * high + low, -1000).astype(jnp.float32)


def whiten_kernel(
    starts_hbm, records_hbm, decimate_hbm, fourier_hbm, smooth_hbm, out, out_one,
    starts, records, decimate, fourier, smooth, raw, done,
):
    pairs = [
        (starts_hbm, starts), (records_hbm, records), (decimate_hbm, decimate),
        (fourier_hbm, fourier), (smooth_hbm, smooth),
    ]
    copies = [pltpu.make_async_copy(a, b, done.at[n]) for n, (a, b) in enumerate(pairs)]
    for copy in copies:
        copy.start()
    copies[0].wait()
    copies[1].wait()
    lane = lax.broadcasted_iota(jnp.int32, (PIECE, LANES), 1)
    used = 5 * GROUP + 1
    last_tile = records.shape[1] // LANES - 1
    for w in range(WINDOWS):
        start = starts[w]
        base = start // LANES
        offset = start % LANES
        turn = (LANES - offset) % LANES
        own = lane < LANES - offset

        def turned(v):
            at = jnp.minimum(base + v, last_tile)
            return pltpu.roll(records[:, pl.ds(pl.multiple_of(at * LANES, LANES), LANES)], turn, 1)

        now = turned(0)
        for v in range(used):
            later = turned(v + 1)
            moved = jnp.where(own, now, later)
            now = later
            run, part = v // 5, v % 5
            if run < GROUP:
                raw[run * 16 + w * 8 : run * 16 + w * 8 + 8, part * LANES : (part + 1) * LANES] = moved
            if part == 0 and run > 0:
                raw[(run - 1) * 16 + w * 8 : (run - 1) * 16 + w * 8 + 8, 5 * LANES :] = moved
    copies[2].wait()
    traces = jnp.dot(raw[...], decimate[...], precision=lax.Precision.HIGHEST, preferred_element_type=jnp.float32)
    parts = small_fourier([(traces[16 * run : 16 * run + 16], None) for run in range(GROUP)])
    left = lax.broadcasted_iota(jnp.int32, (16, LANES), 1) < 64
    copies[3].wait()
    real_tiles, imag_tiles = [], []
    for tile in range(8):
        if tile == 0:
            pair = [parts[0][0], parts[8][0]]
        else:
            pair = list(parts[tile])
        both = jnp.dot(
            jnp.concatenate(pair, axis=1), fourier[tile], precision=lax.Precision.HIGHEST,
            preferred_element_type=jnp.float32,
        )
        real_tiles.append(both[:, :LANES])
        imag_tiles.append(both[:, LANES:])
    reals, imags, powers = [], [], []
    extra = None
    for pair in range(4):
        ra, rb = real_tiles[2 * pair], real_tiles[2 * pair + 1]
        ia, ib = imag_tiles[2 * pair], imag_tiles[2 * pair + 1]
        reals.append(jnp.where(left, ra, rb))
        imags.append(jnp.where(left, ia, ib))
        pa, pb = ra * ra + ia * ia, rb * rb + ib * ib
        powers.append(jnp.where(left, pa, pb))
        extra = plus(extra, jnp.where(left, pb, pa))
    power = jnp.concatenate(powers + [extra], axis=1)
    first = power.astype(jnp.bfloat16)
    rest = power - first.astype(jnp.float32)
    second = rest.astype(jnp.bfloat16)
    third = (rest - second.astype(jnp.float32)).astype(jnp.bfloat16)
    copies[4].wait()
    bins = source_bins()
    window = jnp.concatenate(
        [
            jnp.where(jnp.abs(bins - smooth[0:1, q * LANES : (q + 1) * LANES]) <= HALF, 1.0, 0.0).astype(jnp.bfloat16)
            for q in range(4)
        ],
        axis=1,
    )
    sums = jnp.dot(
        jnp.concatenate([first, second, third], axis=0), window, preferred_element_type=jnp.float32
    )
    smoothed = (sums[:16] + sums[16:32] + sums[32:]) * smooth[1:2, :]
    gain = lax.rsqrt(smoothed + EPS)
    for q, values in enumerate((reals, imags)):
        white = (jnp.concatenate(values, axis=1) * gain).astype(jnp.bfloat16)
        for w in range(WINDOWS):
            out_one[:, (2 * w + q) * FB : (2 * w + q + 1) * FB] = white[8 * w : 8 * w + 8]
            for copy in range(8):
                out[copy, :, (2 * w + q) * FB : (2 * w + q + 1) * FB] = white[8 * w : 8 * w + 8]


def whiten(records, starts):
    decimate = decimation_matrix()
    fourier = fourier_tiles()
    smooth = smoother()
    vmem = pl.BlockSpec(memory_space=pltpu.VMEM)
    hbm = pl.BlockSpec(memory_space=pltpu.HBM)
    return pl.pallas_call(
        whiten_kernel,
        out_shape=(
            jax.ShapeDtypeStruct((8, PIECE, SPEC), jnp.bfloat16),
            jax.ShapeDtypeStruct((PIECE, SPEC), jnp.bfloat16),
        ),
        in_specs=[hbm] * 5,
        out_specs=(vmem, vmem),
        scratch_shapes=[
            pltpu.SMEM((WINDOWS,), jnp.int32),
            pltpu.VMEM(records.shape, jnp.float32),
            pltpu.VMEM(decimate.shape, jnp.float32),
            pltpu.VMEM(fourier.shape, jnp.float32),
            pltpu.VMEM(smooth.shape, jnp.float32),
            pltpu.VMEM((16 * GROUP, 6 * LANES), jnp.float32),
            pltpu.SemaphoreType.DMA((5,)),
        ],
        compiler_params=pltpu.CompilerParams(vmem_limit_bytes=64 * 1024 * 1024 - 512 * 1024),
    )(
        starts, records, jnp.asarray(decimate), jnp.asarray(fourier), jnp.asarray(smooth),
    )


def swap_groups(values):
    lane_group = lax.broadcasted_iota(jnp.int32, values[0].shape, 1) // FINE
    values = list(values)
    for bit in (3, 2, 1, 0):
        distance = 1 << bit
        low_half = (lane_group & distance) == 0
        for a in range(COARSE):
            if a & distance:
                continue
            low, high = values[a], values[a + distance]
            shift = distance * FINE
            values[a] = jnp.where(low_half, low, pltpu.roll(high, shift, 1))
            values[a + distance] = jnp.where(low_half, pltpu.roll(low, LANES - shift, 1), high)
    return values


def turn_sources(own, other, fine, turned, sources):
    src = lax.axis_index("src")
    x, core = src // 4, src % 2
    for side, rows in enumerate((own, other)):

        @pl.loop(0, 8)
        def _(piece):
            place = (x + piece // 2) % 4 * 4 + piece % 2 * 2 + (core if side == 0 else 1 - core)
            sources[...] = rows[piece].astype(jnp.float32)
            for pair in range(PIECE // 2):
                for w in range(WINDOWS):
                    at_w = 2 * w * FB
                    reals, imags = [], []
                    for k in range(2):
                        ch = 2 * pair + k
                        real = jnp.broadcast_to(sources[ch : ch + 1, at_w : at_w + FB], (FINE, FB))
                        imag = jnp.broadcast_to(sources[ch : ch + 1, at_w + FB : at_w + 2 * FB], (FINE, FB))
                        c, s = fine[0], fine[1]
                        reals.append(real * c - imag * s)
                        imags.append(real * s + imag * c)
                    target = pl.ds(pl.multiple_of(place * PIECE * FINE + pair * 16, 16), 16)
                    turned[target, at_w : at_w + FB] = jnp.concatenate(reals, 0).astype(jnp.bfloat16)
                    turned[target, at_w + FB : at_w + 2 * FB] = jnp.concatenate(imags, 0).astype(jnp.bfloat16)


PER = 4


def correlate_kernel(flip, mask, receivers, coarse, *rest):
    step = pl.program_id(0)
    if flip:
        turned, _, out, spread = rest
    else:
        own, other, fine, out, turned, spread, sources = rest

        @pl.when(step == 0)
        def _():
            turn_sources(own, other, fine, turned, sources)

    src, rcv = lax.axis_index("src"), lax.axis_index("rcv")
    y_hi = (rcv + flip) % 2
    for piece in range(PER):
        held = receivers[piece].astype(jnp.float32)
        for w in range(WINDOWS):
            at_w = 2 * w * FB
            real, imag = held[:, at_w : at_w + FB], held[:, at_w + FB : at_w + 2 * FB]
            for pair in range(COARSE // 2):
                reals, imags = [], []
                for k in range(2):
                    lag = 2 * pair + k
                    c = jnp.broadcast_to(coarse[0, lag : lag + 1], (PIECE, FB))
                    s = jnp.broadcast_to(coarse[1, lag : lag + 1], (PIECE, FB))
                    reals.append(real * c - imag * s)
                    imags.append(real * s + imag * c)
                row = piece * COARSE * PIECE + pair * 16
                spread[row : row + 16, at_w : at_w + FB] = jnp.concatenate(reals, 0).astype(jnp.bfloat16)
                spread[row : row + 16, at_w + FB : at_w + 2 * FB] = jnp.concatenate(imags, 0).astype(jnp.bfloat16)

    sublane = lax.broadcasted_iota(jnp.int32, (PIECE, LANES), 0)
    limits = []
    for piece in range(PER):
        block = 2 * (PER * step + piece) + y_hi
        limit = jnp.where(block == rcv, src * PIECE, 4096)
        limits.append(sublane + jnp.where((block >= rcv) & (mask[block] > 0), limit, -4096))
    for chunk in range(4):
        lagged = lax.dot_general(
            spread[...], turned[chunk * 256 : (chunk + 1) * 256, :], (((1,), (1,)), ((), ())),
            preferred_element_type=jnp.float32,
        )
        for piece in range(PER):
            for half in range(2):
                rows = piece * COARSE * PIECE
                values = [
                    lagged[rows + lag * PIECE : rows + (lag + 1) * PIECE, half * LANES : (half + 1) * LANES]
                    for lag in range(COARSE)
                ]
                for k, value in enumerate(swap_groups(values)):
                    source = chunk * 32 + half * 16 + k
                    out[source, piece, 0] = jnp.where(limits[piece] > source, value, 0.0).astype(jnp.bfloat16)


def correlate(mask, receivers, flip, *rest):
    fine = phases(np.arange(FINE), 1.0)
    coarse = phases(-(FINE * np.arange(COARSE) - LAGS // 2), 1.0 / math.sqrt(WINDOWS * FB))
    vmem = pl.BlockSpec(memory_space=pltpu.VMEM)

    def place(i):
        return 0, i, (lax.axis_index("rcv") + flip) % 2, 0, 0

    in_specs = [
        pl.BlockSpec(memory_space=pltpu.SMEM),
        pl.BlockSpec((PER, PIECE, SPEC), lambda i: (i, 0, 0)),
        vmem,
    ]
    result = jax.ShapeDtypeStruct((128, 8, 2, PIECE, LAGS), jnp.bfloat16)
    turned = jax.ShapeDtypeStruct((128 * FINE, SPEC), jnp.bfloat16)
    block = pl.BlockSpec((128, PER, 1, PIECE, LAGS), place)
    spread = pltpu.VMEM((PER * COARSE * PIECE, SPEC), jnp.bfloat16)
    common = dict(
        grid=(8 // PER,),
        cost_estimate=pl.CostEstimate(
            flops=2 * 1024 * 1024 * SPEC, bytes_accessed=6 << 20, transcendentals=0
        ),
        compiler_params=pltpu.CompilerParams(vmem_limit_bytes=24 * 1024 * 1024),
    )
    operands = (mask, receivers, jnp.asarray(coarse)) + rest
    if flip:
        return pl.pallas_call(
            functools.partial(correlate_kernel, flip),
            in_specs=in_specs + [vmem, pl.BlockSpec(memory_space=pltpu.HBM)],
            out_specs=block, out_shape=result, scratch_shapes=[spread],
            input_output_aliases={4: 0}, **common,
        )(*operands)
    return pl.pallas_call(
        functools.partial(correlate_kernel, flip),
        in_specs=in_specs + [vmem] * 3,
        out_specs=(block, vmem), out_shape=(result, turned),
        scratch_shapes=[spread, pltpu.VMEM((PIECE, SPEC), jnp.float32)], **common,
    )(*operands, jnp.asarray(fine))


def move(block, axis, source_of):
    return lax.ppermute(block, axis, [(source_of(i), i) for i in range(lax.axis_size(axis))])


CHIPS = [[core + 2 * k for k in range(8)] for core in range(2)]


def gather_sources(own, near):
    y_lo = lax.axis_index("src") // 2 % 2
    two = jnp.where(y_lo == 0, jnp.stack([own, near]), jnp.stack([near, own]))
    mine = jnp.concatenate([two] + [
        move(two, "src", lambda i, k=k: ((i // 4 + k) % 4) * 4 + i % 4) for k in (1, 2, 3)
    ])
    return mine, move(mine, "src", lambda i: i ^ 1)


def no_sources(own, near):
    return (jnp.zeros((8, PIECE, SPEC), own.dtype),) * 2


def on_device(records, starts, block_mask):
    copies, own = whiten(records, starts)
    near = move(own, "src", lambda i: i ^ 2)
    receivers = lax.all_to_all(copies, "rcv", 0, 0, axis_index_groups=CHIPS)
    mine, other = lax.cond(starts[0] >= 0, gather_sources, no_sources, own, near)
    far = move(receivers, "rcv", lambda i: i ^ 1)
    mask = block_mask.reshape(-1)
    result, turned = correlate(mask, receivers, 0, mine, other)
    result = correlate(mask, far, 1, turned, result)
    return result.reshape(128, BLOCKS, 1, PIECE, LAGS)


def solution(mesh):
    in_specs = (P(("rcv", "src"), None), P(), P("rcv", None, "src"))
    out_specs = P("rcv", None, "src", None, None)
    return jax.shard_map(
        on_device, mesh=mesh, in_specs=in_specs, out_specs=out_specs, check_vma=False
    )
```

```python
import functools
import math

import jax
import jax.numpy as jnp
import ml_dtypes
import numpy as np
from jax import lax
from jax.experimental import pallas as pl
from jax.experimental.pallas import tpu as pltpu
from jax.sharding import PartitionSpec as P

DEC = 5
NT = 2048
FB = 512
HALF = 64
LAGS = 128
TAPS = 65
F = 1024
RAW = 10300
WINDOWS = 2
BLOCKS = 16
PIECE = 8
GROUP = 16
LANES = 128
FINE = 8
COARSE = LAGS // FINE
EPS = 1e-06
SPEC = WINDOWS * 2 * FB


def lowpass():
    k = np.arange(TAPS, dtype=np.float64)
    taper = 0.5 - 0.5 * np.cos(2.0 * np.pi * (k + 1.0) / (TAPS + 1.0))
    return np.sinc((k - (TAPS - 1) / 2.0) / DEC) * taper / DEC


def decimation_matrix():
    taps = lowpass()
    matrix = np.zeros((6 * LANES, LANES))
    for n in range(LANES):
        matrix[DEC * n : DEC * n + TAPS, n] = taps
    return np.concatenate(thirds(matrix), axis=1)


def tile_bins():
    bins = -np.ones((8, LANES), np.int64)
    first = np.zeros((8, LANES), np.int64)
    for tile in range(8):
        pair, side = tile // 2, tile % 2
        for half in range(2):
            low = (0, 8)[half] if tile == 0 else (tile, GROUP - tile)[half]
            for high in range((FB + HALF) // GROUP):
                if high < FB // GROUP:
                    column = side * 64 + half * 32 + high
                else:
                    column = (1 - side) * 64 + pair * 8 + half * 4 + high - FB // GROUP
                bins[tile, column] = GROUP * high + low
                first[tile, column] = half
    return bins, first


def thirds(values):
    parts = []
    rest = values.astype(np.float64)
    for _ in range(3):
        parts.append(rest.astype(np.float32).astype(ml_dtypes.bfloat16))
        rest = rest - parts[-1].astype(np.float64)
    return parts


def fourier_tiles():
    bins, _ = tile_bins()
    angle = 2.0 * np.pi * ((bins[:, None, :] * np.arange(LANES)[None, :, None]) % NT) / NT
    used = bins[:, None, :] >= 0
    return np.stack(thirds(np.concatenate([used * np.cos(angle), used * np.sin(angle)], axis=2)))


def band_bins():
    bins, _ = tile_bins()
    band = []
    extra = -np.ones(LANES, np.int64)
    for pair in range(4):
        left, right = bins[2 * pair], bins[2 * pair + 1]
        band.append(np.where(np.arange(LANES) < 64, left, right))
        swapped = np.where(np.arange(LANES) < 64, right, left)
        extra = np.where(swapped >= 0, swapped, extra)
    return np.concatenate(band), extra


def smoother():
    band, _ = band_bins()
    counted = np.minimum(band + HALF, F - 1) - np.maximum(band - HALF, 0) + 1
    return np.stack([band.astype(np.float32), (1.0 / counted).astype(np.float32)])


def phases(lags, scale):
    band, _ = band_bins()
    angle = 2.0 * np.pi * ((lags[:, None] * band[None, :]) % NT) / NT
    return np.stack([np.cos(angle), np.sin(angle)]).astype(np.float32) * np.float32(scale)


def plus(a, b):
    if a is None:
        return b
    return a if b is None else a + b


def minus(a, b):
    if b is None:
        return a
    return -b if a is None else a - b


def times(a, factor):
    return None if a is None or factor == 0.0 else (a if factor == 1.0 else (-a if factor == -1.0 else a * factor))


def small_fourier(values):
    count = len(values)
    if count == 1:
        return values
    even, odd = small_fourier(values[0::2]), small_fourier(values[1::2])
    low, high = [], []
    for f in range(count // 2):
        angle = 2.0 * math.pi * f / count
        c, s = math.cos(angle), math.sin(angle)
        c = 0.0 if 4 * f == count else c
        real, imag = odd[f]
        turned = (plus(times(real, c), times(imag, s)), minus(times(imag, c), times(real, s)))
        low.append((plus(even[f][0], turned[0]), plus(even[f][1], turned[1])))
        high.append((minus(even[f][0], turned[0]), minus(even[f][1], turned[1])))
    return low + high


def source_bins():
    row = lax.broadcasted_iota(jnp.int32, (5 * LANES, LANES), 0)
    within = row % LANES
    is_band = row < FB
    side = jnp.where(is_band, within // 64, 1 - within // 64)
    pair = jnp.where(is_band, row // LANES, within % 64 // 8)
    half = jnp.where(is_band, within % 64 // 32, within % 8 // 4)
    high = jnp.where(is_band, within % 32, FB // GROUP + within % 4)
    tile = 2 * pair + side
    low = jnp.where(half == 0, tile, jnp.where(tile == 0, GROUP // 2, GROUP - tile))
    used = is_band | (within % 64 < 32)
    return jnp.where(used, GROUP * high + low, -1000).astype(jnp.float32)


def split(values):
    first = values.astype(jnp.bfloat16)
    rest = values - first.astype(jnp.float32)
    second = rest.astype(jnp.bfloat16)
    return [first, second, (rest - second.astype(jnp.float32)).astype(jnp.bfloat16)]


def product(left, right):
    return jnp.dot(left, right, preferred_element_type=jnp.float32)


def whiten_kernel(
    starts_hbm, records_hbm, decimate_hbm, fourier_hbm, smooth_hbm, out, out_one,
    starts, records, decimate, fourier, smooth, raw, done,
):
    pairs = [
        (starts_hbm, starts), (records_hbm, records), (decimate_hbm, decimate),
        (fourier_hbm, fourier), (smooth_hbm, smooth),
    ]
    copies = [pltpu.make_async_copy(a, b, done.at[n]) for n, (a, b) in enumerate(pairs)]
    for copy in copies:
        copy.start()
    copies[0].wait()
    copies[1].wait()
    lane = lax.broadcasted_iota(jnp.int32, (PIECE, LANES), 1)
    used = 5 * GROUP + 1
    last_tile = records.shape[1] // LANES - 1
    for w in range(WINDOWS):
        start = starts[w]
        base = start // LANES
        offset = start % LANES
        turn = (LANES - offset) % LANES
        own = lane < LANES - offset

        def turned(v):
            at = jnp.minimum(base + v, last_tile)
            return pltpu.roll(records[:, pl.ds(pl.multiple_of(at * LANES, LANES), LANES)], turn, 1)

        now = turned(0)
        for v in range(used):
            later = turned(v + 1)
            moved = jnp.where(own, now, later)
            now = later
            run, part = v // 5, v % 5
            if run < GROUP:
                raw[run * 16 + w * 8 : run * 16 + w * 8 + 8, part * LANES : (part + 1) * LANES] = moved
            if part == 0 and run > 0:
                raw[(run - 1) * 16 + w * 8 : (run - 1) * 16 + w * 8 + 8, 5 * LANES :] = moved
    copies[2].wait()
    rows = raw.shape[0]
    parts = split(raw[...])
    wide = product(jnp.concatenate(parts, axis=0), decimate[:, : 2 * LANES])
    traces = product(parts[0], decimate[:, 2 * LANES :])
    traces = traces + wide[2 * rows :, :LANES] + wide[rows : 2 * rows, LANES:]
    traces = traces + (wide[:rows, LANES:] + wide[rows : 2 * rows, :LANES]) + wide[:rows, :LANES]
    parts = small_fourier([(traces[16 * run : 16 * run + 16], None) for run in range(GROUP)])
    lane = lax.broadcasted_iota(jnp.int32, (16, LANES), 1)
    left = lane < 64
    copies[3].wait()
    real_tiles, imag_tiles = [], []
    for tile in range(8):
        pair = (parts[0][0], parts[8][0]) if tile == 0 else parts[tile]
        pieces = split(jnp.concatenate(pair, axis=0))
        both = product(jnp.concatenate(pieces, axis=0), fourier[0, tile])
        middle = product(jnp.concatenate(pieces[:2], axis=0), fourier[1, tile])
        low = product(pieces[0], fourier[2, tile])
        both = low + both[64:] + middle[32:] + (both[32:64] + middle[:32]) + both[:32]
        first_cos, first_sin = both[:16, :LANES], both[:16, LANES:]
        second_cos, second_sin = both[16:, :LANES], both[16:, LANES:]
        upper = jnp.where(lane // 64 == tile % 2, lane % 64 // 32, lane % 8 // 4) == 0
        if tile == 0:
            real_tiles.append(jnp.where(upper, first_cos, second_cos))
            imag_tiles.append(-jnp.where(upper, first_sin, second_sin))
        else:
            real_tiles.append(first_cos + jnp.where(upper, second_sin, -second_sin))
            imag_tiles.append(jnp.where(upper, second_cos, -second_cos) - first_sin)
    reals, imags, powers = [], [], []
    extra = None
    for pair in range(4):
        ra, rb = real_tiles[2 * pair], real_tiles[2 * pair + 1]
        ia, ib = imag_tiles[2 * pair], imag_tiles[2 * pair + 1]
        reals.append(jnp.where(left, ra, rb))
        imags.append(jnp.where(left, ia, ib))
        pa, pb = ra * ra + ia * ia, rb * rb + ib * ib
        powers.append(jnp.where(left, pa, pb))
        extra = plus(extra, jnp.where(left, pb, pa))
    power = jnp.concatenate(powers + [extra], axis=1)
    copies[4].wait()
    bins = source_bins()
    window = jnp.concatenate(
        [
            jnp.where(jnp.abs(bins - smooth[0:1, q * LANES : (q + 1) * LANES]) <= HALF, 1.0, 0.0).astype(jnp.bfloat16)
            for q in range(4)
        ],
        axis=1,
    )
    sums = product(jnp.concatenate(split(power), axis=0), window)
    smoothed = (sums[:16] + sums[16:32] + sums[32:]) * smooth[1:2, :]
    gain = lax.rsqrt(smoothed + EPS)
    for q, values in enumerate((reals, imags)):
        white = (jnp.concatenate(values, axis=1) * gain).astype(jnp.bfloat16)
        for w in range(WINDOWS):
            out_one[:, (2 * w + q) * FB : (2 * w + q + 1) * FB] = white[8 * w : 8 * w + 8]
            for copy in range(8):
                out[copy, :, (2 * w + q) * FB : (2 * w + q + 1) * FB] = white[8 * w : 8 * w + 8]


def whiten(records, starts):
    decimate = decimation_matrix()
    fourier = fourier_tiles()
    smooth = smoother()
    vmem = pl.BlockSpec(memory_space=pltpu.VMEM)
    hbm = pl.BlockSpec(memory_space=pltpu.HBM)
    return pl.pallas_call(
        whiten_kernel,
        out_shape=(
            jax.ShapeDtypeStruct((8, PIECE, SPEC), jnp.bfloat16),
            jax.ShapeDtypeStruct((PIECE, SPEC), jnp.bfloat16),
        ),
        in_specs=[hbm] * 5,
        out_specs=(vmem, vmem),
        scratch_shapes=[
            pltpu.SMEM((WINDOWS,), jnp.int32),
            pltpu.VMEM(records.shape, jnp.float32),
            pltpu.VMEM(decimate.shape, jnp.bfloat16),
            pltpu.VMEM(fourier.shape, jnp.bfloat16),
            pltpu.VMEM(smooth.shape, jnp.float32),
            pltpu.VMEM((16 * GROUP, 6 * LANES), jnp.float32),
            pltpu.SemaphoreType.DMA((5,)),
        ],
        compiler_params=pltpu.CompilerParams(vmem_limit_bytes=64 * 1024 * 1024 - 512 * 1024),
    )(
        starts, records, jnp.asarray(decimate), jnp.asarray(fourier), jnp.asarray(smooth),
    )


def swap_groups(values):
    lane_group = lax.broadcasted_iota(jnp.int32, values[0].shape, 1) // FINE
    values = list(values)
    for bit in (3, 2, 1, 0):
        distance = 1 << bit
        low_half = (lane_group & distance) == 0
        for a in range(COARSE):
            if a & distance:
                continue
            low, high = values[a], values[a + distance]
            shift = distance * FINE
            values[a] = jnp.where(low_half, low, pltpu.roll(high, shift, 1))
            values[a + distance] = jnp.where(low_half, pltpu.roll(low, LANES - shift, 1), high)
    return values


def turn_sources(own, other, fine, turned, sources):
    src = lax.axis_index("src")
    x, core = src // 4, src % 2
    for side, rows in enumerate((own, other)):

        @pl.loop(0, 8)
        def _(piece):
            place = (x + piece // 2) % 4 * 4 + piece % 2 * 2 + (core if side == 0 else 1 - core)
            sources[...] = rows[piece].astype(jnp.float32)
            for pair in range(PIECE // 2):
                for w in range(WINDOWS):
                    at_w = 2 * w * FB
                    reals, imags = [], []
                    for k in range(2):
                        ch = 2 * pair + k
                        real = jnp.broadcast_to(sources[ch : ch + 1, at_w : at_w + FB], (FINE, FB))
                        imag = jnp.broadcast_to(sources[ch : ch + 1, at_w + FB : at_w + 2 * FB], (FINE, FB))
                        c, s = fine[0], fine[1]
                        reals.append(real * c - imag * s)
                        imags.append(real * s + imag * c)
                    target = pl.ds(pl.multiple_of(place * PIECE * FINE + pair * 16, 16), 16)
                    turned[target, at_w : at_w + FB] = jnp.concatenate(reals, 0).astype(jnp.bfloat16)
                    turned[target, at_w + FB : at_w + 2 * FB] = jnp.concatenate(imags, 0).astype(jnp.bfloat16)


PER = 4


def correlate_kernel(flip, mask, receivers, coarse, *rest):
    step = pl.program_id(0)
    if flip:
        turned, _, out, spread = rest
    else:
        own, other, fine, out, turned, spread, sources = rest

        @pl.when(step == 0)
        def _():
            turn_sources(own, other, fine, turned, sources)

    src, rcv = lax.axis_index("src"), lax.axis_index("rcv")
    y_hi = (rcv + flip) % 2
    for couple in range(PER // 2):
        held = []
        for k in range(2):
            block = 2 * (PER * step + 2 * couple + k) + y_hi
            wanted = jnp.where((block >= rcv) & (mask[block] > 0), 1.0, 0.0)
            held.append(receivers[2 * couple + k].astype(jnp.float32) * wanted)
        held = jnp.concatenate(held, axis=0)
        for w in range(WINDOWS):
            at_w = 2 * w * FB
            real, imag = held[:, at_w : at_w + FB], held[:, at_w + FB : at_w + 2 * FB]
            for lag in range(COARSE):
                c = jnp.broadcast_to(coarse[0, lag : lag + 1], (2 * PIECE, FB))
                s = jnp.broadcast_to(coarse[1, lag : lag + 1], (2 * PIECE, FB))
                row = (couple * COARSE + lag) * 2 * PIECE
                spread[row : row + 16, at_w : at_w + FB] = (real * c - imag * s).astype(jnp.bfloat16)
                spread[row : row + 16, at_w + FB : at_w + 2 * FB] = (real * s + imag * c).astype(jnp.bfloat16)

    for chunk in range(4):
        lagged = lax.dot_general(
            spread[...], turned[chunk * 256 : (chunk + 1) * 256, :], (((1,), (1,)), ((), ())),
            preferred_element_type=jnp.float32,
        )
        for couple in range(PER // 2):
            for half in range(2):
                rows = couple * COARSE * 2 * PIECE
                values = [
                    lagged[
                        rows + lag * 2 * PIECE : rows + (lag + 1) * 2 * PIECE, half * LANES : (half + 1) * LANES
                    ].astype(jnp.bfloat16)
                    for lag in range(COARSE)
                ]
                for k, value in enumerate(swap_groups(values)):
                    source = chunk * 32 + half * 16 + k
                    out[source, 2 * couple : 2 * couple + 2] = value.reshape(2, PIECE, LAGS)

    if not flip:
        @pl.when(step == rcv // 2 // PER)
        def _():
            at = rcv // 2 % PER
            receiver = src * PIECE + lax.broadcasted_iota(jnp.int32, (PIECE, LAGS), 0)

            @pl.loop(0, 128)
            def _(source):
                kept = jnp.where(receiver > source, out[source, at].astype(jnp.float32), 0.0)
                out[source, at] = kept.astype(jnp.bfloat16)


def correlate(mask, receivers, flip, *rest):
    fine = phases(np.arange(FINE), 1.0)
    coarse = phases(-(FINE * np.arange(COARSE) - LAGS // 2), 1.0 / math.sqrt(WINDOWS * FB))
    vmem = pl.BlockSpec(memory_space=pltpu.VMEM)

    def place(i):
        return 0, i, (lax.axis_index("rcv") + flip) % 2, 0, 0

    in_specs = [
        pl.BlockSpec(memory_space=pltpu.SMEM),
        pl.BlockSpec((PER, PIECE, SPEC), lambda i: (i, 0, 0)),
        vmem,
    ]
    result = jax.ShapeDtypeStruct((128, 8, 2, PIECE, LAGS), jnp.bfloat16)
    turned = jax.ShapeDtypeStruct((128 * FINE, SPEC), jnp.bfloat16)
    block = pl.BlockSpec((128, PER, None, PIECE, LAGS), place)
    spread = pltpu.VMEM((PER * COARSE * PIECE, SPEC), jnp.bfloat16)
    common = dict(
        grid=(8 // PER,),
        cost_estimate=pl.CostEstimate(
            flops=2 * 1024 * 1024 * SPEC, bytes_accessed=6 << 20, transcendentals=0
        ),
        compiler_params=pltpu.CompilerParams(vmem_limit_bytes=24 * 1024 * 1024),
    )
    operands = (mask, receivers, jnp.asarray(coarse)) + rest
    if flip:
        return pl.pallas_call(
            functools.partial(correlate_kernel, flip),
            in_specs=in_specs + [vmem, pl.BlockSpec(memory_space=pltpu.HBM)],
            out_specs=block, out_shape=result, scratch_shapes=[spread],
            input_output_aliases={4: 0}, **common,
        )(*operands)
    return pl.pallas_call(
        functools.partial(correlate_kernel, flip),
        in_specs=in_specs + [vmem] * 3,
        out_specs=(block, vmem), out_shape=(result, turned),
        scratch_shapes=[spread, pltpu.VMEM((PIECE, SPEC), jnp.float32)], **common,
    )(*operands, jnp.asarray(fine))


def move(block, axis, source_of):
    return lax.ppermute(block, axis, [(source_of(i), i) for i in range(lax.axis_size(axis))])


CHIPS = [[core + 2 * k for k in range(8)] for core in range(2)]


def gather_sources(own, near):
    y_lo = lax.axis_index("src") // 2 % 2
    two = jnp.where(y_lo == 0, jnp.stack([own, near]), jnp.stack([near, own]))
    mine = jnp.concatenate([two] + [
        move(two, "src", lambda i, k=k: ((i // 4 + k) % 4) * 4 + i % 4) for k in (1, 2, 3)
    ])
    return mine, move(mine, "src", lambda i: i ^ 1)


def no_sources(own, near):
    return (jnp.zeros((8, PIECE, SPEC), own.dtype),) * 2


def on_device(records, starts, block_mask):
    copies, own = whiten(records, starts)
    near = move(own, "src", lambda i: i ^ 2)
    receivers = lax.all_to_all(copies, "rcv", 0, 0, axis_index_groups=CHIPS)
    mine, other = lax.cond(starts[0] >= 0, gather_sources, no_sources, own, near)
    far = move(receivers, "rcv", lambda i: i ^ 1)
    mask = block_mask.reshape(-1)
    result, turned = correlate(mask, receivers, 0, mine, other)
    result = correlate(mask, far, 1, turned, result)
    return result.reshape(128, BLOCKS, 1, PIECE, LAGS)


def solution(mesh):
    in_specs = (P(("rcv", "src"), None), P(), P("rcv", None, "src"))
    out_specs = P("rcv", None, "src", None, None)
    return jax.shard_map(
        on_device, mesh=mesh, in_specs=in_specs, out_specs=out_specs, check_vma=False
    )
```

```python
import functools
import math

import jax
import jax.numpy as jnp
import ml_dtypes
import numpy as np
from jax import lax
from jax.experimental import pallas as pl
from jax.experimental.pallas import tpu as pltpu
from jax.sharding import PartitionSpec as P

DEC = 5
NT = 2048
FB = 512
HALF = 64
LAGS = 128
TAPS = 65
F = 1024
RAW = 10300
WINDOWS = 2
BLOCKS = 16
PIECE = 8
GROUP = 16
LANES = 128
FINE = 8
COARSE = LAGS // FINE
EPS = 1e-06
SPEC = WINDOWS * 2 * FB


def lowpass():
    k = np.arange(TAPS, dtype=np.float64)
    taper = 0.5 - 0.5 * np.cos(2.0 * np.pi * (k + 1.0) / (TAPS + 1.0))
    return np.sinc((k - (TAPS - 1) / 2.0) / DEC) * taper / DEC


def decimation_matrix():
    taps = lowpass()
    matrix = np.zeros((6 * LANES, LANES))
    for n in range(LANES):
        matrix[DEC * n : DEC * n + TAPS, n] = taps
    return np.concatenate(thirds(matrix), axis=1)


def tile_bins():
    bins = -np.ones((8, LANES), np.int64)
    first = np.zeros((8, LANES), np.int64)
    for tile in range(8):
        pair, side = tile // 2, tile % 2
        for half in range(2):
            low = (0, 8)[half] if tile == 0 else (tile, GROUP - tile)[half]
            for high in range((FB + HALF) // GROUP):
                if high < FB // GROUP:
                    column = side * 64 + half * 32 + high
                else:
                    column = (1 - side) * 64 + pair * 8 + half * 4 + high - FB // GROUP
                bins[tile, column] = GROUP * high + low
                first[tile, column] = half
    return bins, first


def thirds(values):
    parts = []
    rest = values.astype(np.float64)
    for _ in range(3):
        parts.append(rest.astype(np.float32).astype(ml_dtypes.bfloat16))
        rest = rest - parts[-1].astype(np.float64)
    return parts


def fourier_tiles():
    bins, _ = tile_bins()
    angle = 2.0 * np.pi * ((bins[:, None, :] * np.arange(LANES)[None, :, None]) % NT) / NT
    used = bins[:, None, :] >= 0
    return np.stack(thirds(np.concatenate([used * np.cos(angle), used * np.sin(angle)], axis=2)))


def band_bins():
    bins, _ = tile_bins()
    band = []
    extra = -np.ones(LANES, np.int64)
    for pair in range(4):
        left, right = bins[2 * pair], bins[2 * pair + 1]
        band.append(np.where(np.arange(LANES) < 64, left, right))
        swapped = np.where(np.arange(LANES) < 64, right, left)
        extra = np.where(swapped >= 0, swapped, extra)
    return np.concatenate(band), extra


def smoother():
    band, _ = band_bins()
    counted = np.minimum(band + HALF, F - 1) - np.maximum(band - HALF, 0) + 1
    return np.stack([band.astype(np.float32), (1.0 / counted).astype(np.float32)])


def phases(lags, scale):
    band, _ = band_bins()
    angle = 2.0 * np.pi * ((lags[:, None] * band[None, :]) % NT) / NT
    return np.stack([np.cos(angle), np.sin(angle)]).astype(np.float32) * np.float32(scale)


def plus(a, b):
    if a is None:
        return b
    return a if b is None else a + b


def minus(a, b):
    if b is None:
        return a
    return -b if a is None else a - b


def times(a, factor):
    return None if a is None or factor == 0.0 else (a if factor == 1.0 else (-a if factor == -1.0 else a * factor))


def small_fourier(values):
    count = len(values)
    if count == 1:
        return values
    even, odd = small_fourier(values[0::2]), small_fourier(values[1::2])
    low, high = [], []
    for f in range(count // 2):
        angle = 2.0 * math.pi * f / count
        c, s = math.cos(angle), math.sin(angle)
        c = 0.0 if 4 * f == count else c
        real, imag = odd[f]
        turned = (plus(times(real, c), times(imag, s)), minus(times(imag, c), times(real, s)))
        low.append((plus(even[f][0], turned[0]), plus(even[f][1], turned[1])))
        high.append((minus(even[f][0], turned[0]), minus(even[f][1], turned[1])))
    return low + high


def source_bins():
    row = lax.broadcasted_iota(jnp.int32, (5 * LANES, LANES), 0)
    within = row % LANES
    is_band = row < FB
    side = jnp.where(is_band, within // 64, 1 - within // 64)
    pair = jnp.where(is_band, row // LANES, within % 64 // 8)
    half = jnp.where(is_band, within % 64 // 32, within % 8 // 4)
    high = jnp.where(is_band, within % 32, FB // GROUP + within % 4)
    tile = 2 * pair + side
    low = jnp.where(half == 0, tile, jnp.where(tile == 0, GROUP // 2, GROUP - tile))
    used = is_band | (within % 64 < 32)
    return jnp.where(used, GROUP * high + low, -1000).astype(jnp.float32)


def split(values):
    first = values.astype(jnp.bfloat16)
    rest = values - first.astype(jnp.float32)
    second = rest.astype(jnp.bfloat16)
    return [first, second, (rest - second.astype(jnp.float32)).astype(jnp.bfloat16)]


def product(left, right):
    return jnp.dot(left, right, preferred_element_type=jnp.float32)


def whiten_kernel(
    starts_hbm, records_hbm, decimate_hbm, fourier_hbm, smooth_hbm, out, out_one,
    starts, records, decimate, fourier, smooth, raw, done,
):
    pairs = [
        (starts_hbm, starts), (records_hbm, records), (decimate_hbm, decimate),
        (fourier_hbm, fourier), (smooth_hbm, smooth),
    ]
    copies = [pltpu.make_async_copy(a, b, done.at[n]) for n, (a, b) in enumerate(pairs)]
    for copy in copies:
        copy.start()
    copies[0].wait()
    copies[1].wait()
    lane = lax.broadcasted_iota(jnp.int32, (PIECE, LANES), 1)
    used = 5 * GROUP + 1
    last_tile = records.shape[1] // LANES - 1
    for w in range(WINDOWS):
        start = starts[w]
        base = start // LANES
        offset = start % LANES
        turn = (LANES - offset) % LANES
        own = lane < LANES - offset

        def turned(v):
            at = jnp.minimum(base + v, last_tile)
            return pltpu.roll(records[:, pl.ds(pl.multiple_of(at * LANES, LANES), LANES)], turn, 1)

        now = turned(0)
        for v in range(used):
            later = turned(v + 1)
            moved = jnp.where(own, now, later)
            now = later
            run, part = v // 5, v % 5
            if run < GROUP:
                raw[run * 16 + w * 8 : run * 16 + w * 8 + 8, part * LANES : (part + 1) * LANES] = moved
            if part == 0 and run > 0:
                raw[(run - 1) * 16 + w * 8 : (run - 1) * 16 + w * 8 + 8, 5 * LANES :] = moved
    copies[2].wait()
    rows = raw.shape[0]
    parts = split(raw[...])
    wide = product(jnp.concatenate(parts, axis=0), decimate[:, : 2 * LANES])
    traces = product(parts[0], decimate[:, 2 * LANES :])
    traces = traces + wide[2 * rows :, :LANES] + wide[rows : 2 * rows, LANES:]
    traces = traces + (wide[:rows, LANES:] + wide[rows : 2 * rows, :LANES]) + wide[:rows, :LANES]
    parts = small_fourier([(traces[16 * run : 16 * run + 16], None) for run in range(GROUP)])
    lane = lax.broadcasted_iota(jnp.int32, (16, LANES), 1)
    left = lane < 64
    copies[3].wait()
    real_tiles, imag_tiles = [], []
    for tile in range(8):
        pair = (parts[0][0], parts[8][0]) if tile == 0 else parts[tile]
        pieces = split(jnp.concatenate(pair, axis=0))
        both = product(jnp.concatenate(pieces, axis=0), fourier[0, tile])
        middle = product(jnp.concatenate(pieces[:2], axis=0), fourier[1, tile])
        low = product(pieces[0], fourier[2, tile])
        both = low + both[64:] + middle[32:] + (both[32:64] + middle[:32]) + both[:32]
        first_cos, first_sin = both[:16, :LANES], both[:16, LANES:]
        second_cos, second_sin = both[16:, :LANES], both[16:, LANES:]
        upper = jnp.where(lane // 64 == tile % 2, lane % 64 // 32, lane % 8 // 4) == 0
        if tile == 0:
            real_tiles.append(jnp.where(upper, first_cos, second_cos))
            imag_tiles.append(-jnp.where(upper, first_sin, second_sin))
        else:
            real_tiles.append(first_cos + jnp.where(upper, second_sin, -second_sin))
            imag_tiles.append(jnp.where(upper, second_cos, -second_cos) - first_sin)
    reals, imags, powers = [], [], []
    extra = None
    for pair in range(4):
        ra, rb = real_tiles[2 * pair], real_tiles[2 * pair + 1]
        ia, ib = imag_tiles[2 * pair], imag_tiles[2 * pair + 1]
        reals.append(jnp.where(left, ra, rb))
        imags.append(jnp.where(left, ia, ib))
        pa, pb = ra * ra + ia * ia, rb * rb + ib * ib
        powers.append(jnp.where(left, pa, pb))
        extra = plus(extra, jnp.where(left, pb, pa))
    power = jnp.concatenate(powers + [extra], axis=1)
    copies[4].wait()
    bins = source_bins()
    window = jnp.concatenate(
        [
            jnp.where(jnp.abs(bins - smooth[0:1, q * LANES : (q + 1) * LANES]) <= HALF, 1.0, 0.0).astype(jnp.bfloat16)
            for q in range(4)
        ],
        axis=1,
    )
    sums = product(jnp.concatenate(split(power), axis=0), window)
    smoothed = (sums[:16] + sums[16:32] + sums[32:]) * smooth[1:2, :]
    gain = lax.rsqrt(smoothed + EPS)
    for q, values in enumerate((reals, imags)):
        white = (jnp.concatenate(values, axis=1) * gain).astype(jnp.bfloat16)
        for w in range(WINDOWS):
            out_one[:, (2 * w + q) * FB : (2 * w + q + 1) * FB] = white[8 * w : 8 * w + 8]
            for copy in range(8):
                out[copy, :, (2 * w + q) * FB : (2 * w + q + 1) * FB] = white[8 * w : 8 * w + 8]


def whiten(records, starts):
    decimate = decimation_matrix()
    fourier = fourier_tiles()
    smooth = smoother()
    vmem = pl.BlockSpec(memory_space=pltpu.VMEM)
    hbm = pl.BlockSpec(memory_space=pltpu.HBM)
    return pl.pallas_call(
        whiten_kernel,
        out_shape=(
            jax.ShapeDtypeStruct((8, PIECE, SPEC), jnp.bfloat16),
            jax.ShapeDtypeStruct((PIECE, SPEC), jnp.bfloat16),
        ),
        in_specs=[hbm] * 5,
        out_specs=(vmem, vmem),
        scratch_shapes=[
            pltpu.SMEM((WINDOWS,), jnp.int32),
            pltpu.VMEM(records.shape, jnp.float32),
            pltpu.VMEM(decimate.shape, jnp.bfloat16),
            pltpu.VMEM(fourier.shape, jnp.bfloat16),
            pltpu.VMEM(smooth.shape, jnp.float32),
            pltpu.VMEM((16 * GROUP, 6 * LANES), jnp.float32),
            pltpu.SemaphoreType.DMA((5,)),
        ],
        compiler_params=pltpu.CompilerParams(vmem_limit_bytes=64 * 1024 * 1024 - 512 * 1024),
    )(
        starts, records, jnp.asarray(decimate), jnp.asarray(fourier), jnp.asarray(smooth),
    )


def swap_groups(values):
    lane_group = lax.broadcasted_iota(jnp.int32, values[0].shape, 1) // FINE
    values = list(values)
    for bit in (3, 2, 1, 0):
        distance = 1 << bit
        low_half = (lane_group & distance) == 0
        for a in range(COARSE):
            if a & distance:
                continue
            low, high = values[a], values[a + distance]
            shift = distance * FINE
            values[a] = jnp.where(low_half, low, pltpu.roll(high, shift, 1))
            values[a + distance] = jnp.where(low_half, pltpu.roll(low, LANES - shift, 1), high)
    return values


def turn_sources(own, other, fine, turned, sources):
    src = lax.axis_index("src")
    x, core = src // 4, src % 2
    for side, rows in enumerate((own, other)):

        @pl.loop(0, 8)
        def _(piece):
            place = (x + piece // 2) % 4 * 4 + piece % 2 * 2 + (core if side == 0 else 1 - core)
            sources[...] = rows[piece].astype(jnp.float32)
            for pair in range(PIECE // 2):
                for w in range(WINDOWS):
                    at_w = 2 * w * FB
                    reals, imags = [], []
                    for k in range(2):
                        ch = 2 * pair + k
                        real = jnp.broadcast_to(sources[ch : ch + 1, at_w : at_w + FB], (FINE, FB))
                        imag = jnp.broadcast_to(sources[ch : ch + 1, at_w + FB : at_w + 2 * FB], (FINE, FB))
                        c, s = fine[0], fine[1]
                        reals.append(real * c - imag * s)
                        imags.append(real * s + imag * c)
                    target = pl.ds(pl.multiple_of(place * PIECE * FINE + pair * 16, 16), 16)
                    turned[target, at_w : at_w + FB] = jnp.concatenate(reals, 0).astype(jnp.bfloat16)
                    turned[target, at_w + FB : at_w + 2 * FB] = jnp.concatenate(imags, 0).astype(jnp.bfloat16)


PER = 4


def correlate_kernel(flip, mask, receivers, coarse, *rest):
    step = pl.program_id(0)
    if flip:
        turned, _, out, spread = rest
    else:
        own, other, fine, out, turned, spread, sources = rest

        @pl.when(step == 0)
        def _():
            turn_sources(own, other, fine, turned, sources)

    src, rcv = lax.axis_index("src"), lax.axis_index("rcv")
    y_hi = (rcv + flip) % 2
    limits = []
    for couple in range(PER // 2):
        held, limit = [], []
        for k in range(2):
            block = 2 * (PER * step + 2 * couple + k) + y_hi
            wanted = jnp.where((block >= rcv) & (mask[block] > 0), 1.0, 0.0)
            held.append(receivers[2 * couple + k].astype(jnp.float32) * wanted)
            channel = lax.broadcasted_iota(jnp.int32, (PIECE, LANES), 0) + src * PIECE
            limit.append(jnp.where(block == rcv, channel, 4096).astype(jnp.float32))
        limits.append(jnp.concatenate(limit, axis=0).astype(jnp.bfloat16))
        held = jnp.concatenate(held, axis=0)
        for w in range(WINDOWS):
            at_w = 2 * w * FB
            real, imag = held[:, at_w : at_w + FB], held[:, at_w + FB : at_w + 2 * FB]
            for lag in range(COARSE):
                c = jnp.broadcast_to(coarse[0, lag : lag + 1], (2 * PIECE, FB))
                s = jnp.broadcast_to(coarse[1, lag : lag + 1], (2 * PIECE, FB))
                row = (couple * COARSE + lag) * 2 * PIECE
                spread[row : row + 16, at_w : at_w + FB] = (real * c - imag * s).astype(jnp.bfloat16)
                spread[row : row + 16, at_w + FB : at_w + 2 * FB] = (real * s + imag * c).astype(jnp.bfloat16)

    for chunk in range(4):
        lagged = lax.dot_general(
            spread[...], turned[chunk * 256 : (chunk + 1) * 256, :], (((1,), (1,)), ((), ())),
            preferred_element_type=jnp.float32,
        )
        for couple in range(PER // 2):
            for half in range(2):
                rows = couple * COARSE * 2 * PIECE
                values = [
                    lagged[
                        rows + lag * 2 * PIECE : rows + (lag + 1) * 2 * PIECE, half * LANES : (half + 1) * LANES
                    ].astype(jnp.bfloat16)
                    for lag in range(COARSE)
                ]
                for k, value in enumerate(swap_groups(values)):
                    source = chunk * 32 + half * 16 + k
                    if not flip:
                        value = value * jnp.clip(limits[couple] - source, 0, 1)
                    out[source, 2 * couple : 2 * couple + 2] = value.reshape(2, PIECE, LAGS)


def correlate(mask, receivers, flip, *rest):
    fine = phases(np.arange(FINE), 1.0)
    coarse = phases(-(FINE * np.arange(COARSE) - LAGS // 2), 1.0 / math.sqrt(WINDOWS * FB))
    vmem = pl.BlockSpec(memory_space=pltpu.VMEM)

    def place(i):
        return 0, i, (lax.axis_index("rcv") + flip) % 2, 0, 0

    in_specs = [
        pl.BlockSpec(memory_space=pltpu.SMEM),
        pl.BlockSpec((PER, PIECE, SPEC), lambda i: (i, 0, 0)),
        vmem,
    ]
    result = jax.ShapeDtypeStruct((128, 8, 2, PIECE, LAGS), jnp.bfloat16)
    turned = jax.ShapeDtypeStruct((128 * FINE, SPEC), jnp.bfloat16)
    block = pl.BlockSpec((128, PER, None, PIECE, LAGS), place)
    spread = pltpu.VMEM((PER * COARSE * PIECE, SPEC), jnp.bfloat16)
    common = dict(
        grid=(8 // PER,),
        cost_estimate=pl.CostEstimate(
            flops=2 * 1024 * 1024 * SPEC, bytes_accessed=6 << 20, transcendentals=0
        ),
        compiler_params=pltpu.CompilerParams(vmem_limit_bytes=24 * 1024 * 1024),
    )
    operands = (mask, receivers, jnp.asarray(coarse)) + rest
    if flip:
        return pl.pallas_call(
            functools.partial(correlate_kernel, flip),
            in_specs=in_specs + [vmem, pl.BlockSpec(memory_space=pltpu.HBM)],
            out_specs=block, out_shape=result, scratch_shapes=[spread],
            input_output_aliases={4: 0}, **common,
        )(*operands)
    return pl.pallas_call(
        functools.partial(correlate_kernel, flip),
        in_specs=in_specs + [vmem] * 3,
        out_specs=(block, vmem), out_shape=(result, turned),
        scratch_shapes=[spread, pltpu.VMEM((PIECE, SPEC), jnp.float32)], **common,
    )(*operands, jnp.asarray(fine))


def move(block, axis, source_of):
    return lax.ppermute(block, axis, [(source_of(i), i) for i in range(lax.axis_size(axis))])


CHIPS = [[core + 2 * k for k in range(8)] for core in range(2)]


def gather_sources(own, near):
    y_lo = lax.axis_index("src") // 2 % 2
    two = jnp.where(y_lo == 0, jnp.stack([own, near]), jnp.stack([near, own]))
    return jnp.concatenate([two] + [
        move(two, "src", lambda i, k=k: ((i // 4 + k) % 4) * 4 + i % 4) for k in (1, 2, 3)
    ])


def no_sources(own, near):
    return jnp.zeros((8, PIECE, SPEC), own.dtype)


def on_device(records, starts, block_mask):
    copies, own = whiten(records, starts)
    near = move(own, "src", lambda i: i ^ 2)
    receivers = lax.all_to_all(copies, "rcv", 0, 0, axis_index_groups=CHIPS)
    mine = lax.cond(starts[0] >= 0, gather_sources, no_sources, own, near)
    other = move(mine, "src", lambda i: i ^ 1)
    far = move(receivers, "rcv", lambda i: i ^ 1)
    mask = block_mask.reshape(-1)
    result, turned = correlate(mask, receivers, 0, mine, other)
    result = correlate(mask, far, 1, turned, result)
    return result.reshape(128, BLOCKS, 1, PIECE, LAGS)


def solution(mesh):
    in_specs = (P(("rcv", "src"), None), P(), P("rcv", None, "src"))
    out_specs = P("rcv", None, "src", None, None)
    return jax.shard_map(
        on_device, mesh=mesh, in_specs=in_specs, out_specs=out_specs, check_vma=False
    )
```
